32 devices in a mesh: group: 2 (over y), fsdp: 2 (over core), tensor: 8 (over z, x).
Axes of the slice: x: 2, y: 2, z: 4, core: 2. Of those that a mesh axis runs over, the one named last changes fastest.
Arguments:
- step_token_rows: int32 [4, 4], P('group'), parts along dimension 0, may hold values from 0 to 9599
- token_embedding_table: bfloat16 [9600, 5120], P(('fsdp', 'tensor')), may hold values from -3 to 3
- cached_row_lengths: int32 [4], P(('group', 'fsdp')), parts along dimension 0, may hold values from 1024 to 4096, as said below
- key_value_cache: bfloat16 [4, 4096, 2048], P(('group', 'fsdp'), 'tensor'), parts along dimension 0, may hold values from -120 to 120, as said below
- input_norm_gain: bfloat16 [5120], replicated, may hold values from 0.5 to 1.5
- query_key_gains: float32 [2, 128], replicated, may hold values from 1.2 to 2.5
- wqkv: bfloat16 [5120, 10240], P('tensor'), may hold values from -0.078125 to 0.078125
- wout: bfloat16 [8192, 5120], P('tensor'), may hold values from -0.0625 to 0.0625
- adapter_down_projections: bfloat16 [5120, 384], P('tensor'), may hold values from -0.078125 to 0.078125
- adapter_down_output: bfloat16 [8192, 128], P('tensor'), may hold values from -0.0625 to 0.0625
- adapter_up_factors: bfloat16 [128, 15360], P(None, ('fsdp', 'tensor')), may hold values from -0.25 to 0.25
Outputs:
- hidden_out: bfloat16 [4, 4, 5120], P(('group', 'fsdp')), parts along dimension 0
The draws below stay inside these ranges and needn't reach their ends.
There are 2 independent parts, one for each index of `group`. The reference program is written for one: setup_inputs(seed, part) draws one part's arguments, and reference() takes and returns one part's arrays. A program takes and returns all parts, laid end to end along the dimension named above; an argument that names none is the same for every part. Nothing has to cross between parts.
Inputs may be any that keep to these rules, and one draw needn't show every extreme that they name: Row b's cache holds valid entries at its first cached_row_lengths[b] positions only; in every draw some row holds all 4096. `key_value_cache`: entries at positions at or after a row's length are not read.
All inputs are finite; a program needn't handle non-finite values.
Results may differ from the reference program's by a relative error of at most 0.035.
Values may be sent and summed in bfloat16 or wider, within the bound.
A program may use at most 192 MiB of HBM per device.

```python
import math
import jax
import jax.numpy as jnp
from jax import lax

MODEL_DIM = 5120
QUERY_HEADS = 64
KVH = 8
HEAD_SIZE = 128
ADAPTER_RANK = 128
LEN = 4096
STEPS = 4
ROWS = 2
PROJECTION_COLS = 10240
VOCAB = 9600


def draw_cached_row_lengths(key, part):
    key = jax.random.fold_in(key, 1)
    key_row, key_len = jax.random.split(key)
    filled = jax.random.randint(key_len, (ROWS,), LEN // 4, LEN + 1)
    chosen = jax.random.randint(key_row, (), 0, ROWS)
    return jnp.where(jnp.arange(ROWS) == chosen, LEN, filled).astype(jnp.int32)


def draw_key_value_cache(key, part):
    key = jax.random.fold_in(key, 2)
    key_a, key_b = jax.random.split(key, 2)
    key_value_width = KVH * HEAD_SIZE
    key_part = 1.7 * jax.random.normal(key_a, (ROWS, LEN, key_value_width), jnp.float32)
    value_part = jax.random.normal(key_b, (ROWS, LEN, key_value_width), jnp.float32)
    joined = jnp.concatenate([key_part, value_part], axis=-1)
    return jnp.clip(joined, -120.0, 120.0).astype(jnp.bfloat16)


def place_ends(drawn, key, least, top_value):
    shape = drawn.shape
    index_at = [jax.random.randint(jax.random.fold_in(key, axis), (), 0, shape[axis]) for axis in range(len(shape))]
    drawn = drawn.at[tuple(index_at)].set(least)
    longest = shape.index(max(shape))
    index_at[longest] = (index_at[longest] + 1) % shape[longest]
    return drawn.at[tuple(index_at)].set(top_value)


def block_levels(own_key, extent, pieces, smallest, high):
    def one(dim, blocks):
        steps = jax.random.uniform(jax.random.fold_in(jax.random.fold_in(own_key, 6), dim), (blocks,), jnp.float32, smallest / len(pieces), high / len(pieces))
        return jnp.repeat(jnp.exp(steps), extent[dim] // blocks).reshape((-1,) + (1,) * (len(extent) - dim - 1))

    level = one(*pieces[0])
    for cut in pieces[1:]:
        level = level * one(*cut)
    return level


def centred(rng, extent, deviation, limit, pieces=(), held_as=jnp.bfloat16):
    loudness = block_levels(rng, extent, pieces, -0.22, 0.18) if pieces else 1.0
    values = jax.random.normal(rng, extent, jnp.float32) * deviation * loudness
    return jnp.minimum(jnp.maximum(values, -limit), limit).astype(held_as)


def setup_inputs(seed: int = 0, part: int = 0) -> dict:
    streams_of = jax.random.split(jax.random.key(seed), 12)
    part_splits = jax.random.split(jax.random.fold_in(streams_of[11], part), 12)
    step_token_rows = place_ends(jax.random.randint(part_splits[0], (ROWS, STEPS), 0, VOCAB), jax.random.fold_in(part_splits[0], 1), 0, VOCAB - 1).astype(jnp.int32)
    token_embedding_table = centred(streams_of[1], (VOCAB, MODEL_DIM), 0.5, 3.0, ((0, 16),))
    cached_row_lengths = draw_cached_row_lengths(jax.random.fold_in(jax.random.fold_in(streams_of[11], part), 71), part)
    key_value_cache = draw_key_value_cache(jax.random.fold_in(jax.random.fold_in(streams_of[11], part), 71), part)
    input_norm_gain = jnp.clip(1.0 + 0.1 * jax.random.normal(streams_of[4], (MODEL_DIM,), jnp.float32), 0.5, 1.5).astype(jnp.bfloat16)
    query_key_gains = jnp.clip(jnp.exp(jax.random.uniform(streams_of[5], (2, HEAD_SIZE), jnp.float32, math.log(1.2), math.log(2.5))), 1.2, 2.5)
    wqkv = centred(streams_of[6], (MODEL_DIM, PROJECTION_COLS), MODEL_DIM ** -0.5, 0.078125, ((0, 8),))
    wout = centred(streams_of[7], (QUERY_HEADS * HEAD_SIZE, MODEL_DIM), (QUERY_HEADS * HEAD_SIZE) ** -0.5, 0.0625, ((0, 8),))
    adapter_down_projections = centred(streams_of[8], (MODEL_DIM, 3 * ADAPTER_RANK), MODEL_DIM ** -0.5, 0.078125, ((0, 8),))
    adapter_down_output = centred(streams_of[9], (QUERY_HEADS * HEAD_SIZE, ADAPTER_RANK), (QUERY_HEADS * HEAD_SIZE) ** -0.5, 0.0625, ((0, 8),))
    adapter_up_factors = centred(streams_of[10], (ADAPTER_RANK, PROJECTION_COLS + MODEL_DIM), (4 * ADAPTER_RANK) ** -0.5, 0.25, ((1, 16),))
    return dict(step_token_rows=step_token_rows, token_embedding_table=token_embedding_table, cached_row_lengths=cached_row_lengths, key_value_cache=key_value_cache, input_norm_gain=input_norm_gain, query_key_gains=query_key_gains, wqkv=wqkv, wout=wout, adapter_down_projections=adapter_down_projections, adapter_down_output=adapter_down_output, adapter_up_factors=adapter_up_factors)


EPSILON = 1e-06
ROPE_BASE = 1000000.0
ADAPTER_SCALE = 2.0

def rms_scale(values, gain):
    return values * lax.rsqrt(lax.optimization_barrier(jnp.mean(values * values, axis=-1, keepdims=True)) + EPSILON) * gain

def rotate(values, position):
    half_width = values.shape[-1] // 2
    inverse = ROPE_BASE ** (-(2.0 * jnp.arange(half_width, dtype=jnp.float32)) / values.shape[-1])
    angle = position[..., None] * inverse
    cosine = jnp.cos(angle)
    sine = jnp.sin(angle)
    first_half = values[..., :half_width]
    second_half = values[..., half_width:]
    return jnp.concatenate([first_half * cosine - second_half * sine, second_half * cosine + first_half * sine], axis=-1)

def attend_row(packed):
    query_row, cached, length, new_keys, new_values = packed
    groups = QUERY_HEADS // KVH
    key_value_width = KVH * HEAD_SIZE
    scaling = 1.0 / math.sqrt(HEAD_SIZE)
    query_grid = query_row.astype(jnp.float32).reshape(KVH, groups, HEAD_SIZE)
    cache_keys = cached[:, :key_value_width].astype(jnp.float32).reshape(LEN, KVH, HEAD_SIZE)
    cache_values = cached[:, key_value_width:].astype(jnp.float32).reshape(LEN, KVH, HEAD_SIZE)
    scores = jnp.einsum('grd,jgd->grj', query_grid, cache_keys) * scaling
    fresh_scores = jnp.einsum('grd,sgd->grs', query_grid, new_keys.astype(jnp.float32)) * scaling
    visible = jnp.arange(LEN) < length
    largest = jnp.maximum(lax.optimization_barrier(jnp.max(jnp.where(visible, scores, -1e+30), axis=-1)), lax.optimization_barrier(jnp.max(fresh_scores, axis=-1)))
    weights = jnp.where(visible, jnp.exp(scores - largest[..., None]), 0.0)
    fresh_weights = jnp.exp(fresh_scores - largest[..., None])
    denominator = lax.optimization_barrier(jnp.sum(weights, axis=-1)) + lax.optimization_barrier(jnp.sum(fresh_weights, axis=-1))
    rounded = lax.optimization_barrier(weights.astype(jnp.bfloat16)).astype(jnp.float32)
    fresh_rounded = lax.optimization_barrier(fresh_weights.astype(jnp.bfloat16)).astype(jnp.float32)
    numerator = jnp.einsum('grj,jgd->grd', rounded, cache_values)
    numerator = numerator + jnp.einsum('grs,sgd->grd', fresh_rounded, new_values.astype(jnp.float32))
    return (numerator / denominator[..., None]).reshape(QUERY_HEADS * HEAD_SIZE).astype(jnp.bfloat16)

def reference(step_token_rows, token_embedding_table, cached_row_lengths, key_value_cache, input_norm_gain, query_key_gains, wqkv, wout, adapter_down_projections, adapter_down_output, adapter_up_factors):
    query_width = QUERY_HEADS * HEAD_SIZE
    key_value_width = KVH * HEAD_SIZE
    projection_width = query_width + 2 * key_value_width
    weight_delta = jnp.concatenate([jnp.dot(adapter_down_projections[:, :ADAPTER_RANK], adapter_up_factors[:, :query_width], preferred_element_type=jnp.float32), jnp.dot(adapter_down_projections[:, ADAPTER_RANK:2 * ADAPTER_RANK], adapter_up_factors[:, query_width:query_width + key_value_width], preferred_element_type=jnp.float32), jnp.dot(adapter_down_projections[:, 2 * ADAPTER_RANK:], adapter_up_factors[:, query_width + key_value_width:projection_width], preferred_element_type=jnp.float32)], axis=1)
    merged_projection_weight = (wqkv.astype(jnp.float32) + ADAPTER_SCALE * weight_delta).astype(jnp.bfloat16)
    output_weight_delta = jnp.dot(adapter_down_output, adapter_up_factors[:, projection_width:], preferred_element_type=jnp.float32)
    merged_output_weight = (wout.astype(jnp.float32) + ADAPTER_SCALE * output_weight_delta).astype(jnp.bfloat16)
    embedded = token_embedding_table[step_token_rows].astype(jnp.float32)
    key_list = []
    value_list = []
    results = []
    for decode_step in range(STEPS):
        inputs = embedded[:, decode_step]
        normed = rms_scale(inputs, input_norm_gain.astype(jnp.float32)).astype(jnp.bfloat16)
        projected = jnp.dot(normed, merged_projection_weight, preferred_element_type=jnp.float32).astype(jnp.bfloat16)
        queries = projected[:, :query_width].astype(jnp.float32).reshape(ROWS, QUERY_HEADS, HEAD_SIZE)
        new_key = projected[:, query_width:query_width + key_value_width].astype(jnp.float32).reshape(ROWS, KVH, HEAD_SIZE)
        new_value = projected[:, query_width + key_value_width:].reshape(ROWS, KVH, HEAD_SIZE)
        position = (cached_row_lengths + decode_step).astype(jnp.float32)[:, None]
        rotated_query = rotate(rms_scale(queries, query_key_gains[0]), position).astype(jnp.bfloat16)
        key_list.append(rotate(rms_scale(new_key, query_key_gains[1]), position).astype(jnp.bfloat16))
        value_list.append(new_value)
        attended = lax.map(attend_row, (rotated_query, key_value_cache, cached_row_lengths, jnp.stack(key_list, axis=1), jnp.stack(value_list, axis=1)))
        output = jnp.dot(attended, merged_output_weight, preferred_element_type=jnp.float32)
        results.append((inputs + output).astype(jnp.bfloat16))
    return jnp.stack(results, axis=1)
```

```python
import math

import jax
import jax.numpy as jnp
from jax import lax
from jax.experimental import pallas as pl
from jax.experimental.pallas import tpu as pltpu
from jax.sharding import PartitionSpec as P

QUERY_HEADS = 64
KVH = 8
HEAD_SIZE = 128
ADAPTER_RANK = 128
STEPS = 4


EPSILON = 1e-06
ROPE_BASE = 1000000.0
ADAPTER_SCALE = 2.0


def combined_all(x, axis, join):
    gathered = jax.tree.map(
        lambda a, kind: lax.all_gather(a.astype(kind), axis),
        x,
        (jnp.bfloat16, jnp.bfloat16, jnp.bfloat16),
    )

    def take(source):
        return jax.tree.map(
            lambda a, own: lax.dynamic_index_in_dim(a, source, 0, False).astype(own.dtype),
            gathered,
            x,
        )

    return lax.fori_loop(
        1, lax.axis_size(axis), lambda source, state: join(state, take(source)), take(0)
    )


def rms_scale(values, gain):
    return values * lax.rsqrt(jnp.mean(values * values, axis=-1, keepdims=True) + EPSILON) * gain


def rotate(values, position):
    half_width = values.shape[-1] // 2
    inverse = ROPE_BASE ** (-(2.0 * jnp.arange(half_width, dtype=jnp.float32)) / values.shape[-1])
    angle = position[..., None] * inverse
    cosine = jnp.cos(angle)
    sine = jnp.sin(angle)
    first_half = values[..., :half_width]
    second_half = values[..., half_width:]
    return jnp.concatenate(
        [first_half * cosine - second_half * sine, second_half * cosine + first_half * sine],
        axis=-1,
    )


def fold_parts(earlier, later):
    top = jnp.maximum(earlier[0], later[0])
    scale_one = jnp.exp(earlier[0] - top)
    scale_two = jnp.exp(later[0] - top)
    return (
        top,
        earlier[1] * scale_one + later[1] * scale_two,
        earlier[2] * scale_one[..., None] + later[2] * scale_two[..., None],
    )


def local(
    step_token_rows,
    token_embedding_table,
    cached_row_lengths,
    key_value_cache,
    input_norm_gain,
    query_key_gains,
    wqkv,
    wout,
    adapter_down_projections,
    adapter_down_output,
    adapter_up_factors,
):
    tensor_count = lax.axis_size("tensor")
    tensor_index = lax.axis_index("tensor")
    fsdp_index = lax.axis_index("fsdp")
    rows_here = cached_row_lengths.shape[0]
    heads_here = QUERY_HEADS // tensor_count
    slots_here = key_value_cache.shape[1]
    groups = QUERY_HEADS // KVH
    query_width = QUERY_HEADS * HEAD_SIZE
    key_value_width = KVH * HEAD_SIZE
    projection_width = wqkv.shape[1]
    model_width = token_embedding_table.shape[1]
    scaling = 1.0 / math.sqrt(HEAD_SIZE)
    adapter_up_whole = lax.all_gather(adapter_up_factors, ("fsdp", "tensor"), axis=1, tiled=True)
    weight_delta = jnp.concatenate(
        [
            jnp.dot(
                adapter_down_projections[:, :ADAPTER_RANK],
                adapter_up_whole[:, :query_width],
                preferred_element_type=jnp.float32,
            ),
            jnp.dot(
                adapter_down_projections[:, ADAPTER_RANK : 2 * ADAPTER_RANK],
                adapter_up_whole[:, query_width : query_width + key_value_width],
                preferred_element_type=jnp.float32,
            ),
            jnp.dot(
                adapter_down_projections[:, 2 * ADAPTER_RANK :],
                adapter_up_whole[:, query_width + key_value_width : projection_width],
                preferred_element_type=jnp.float32,
            ),
        ],
        axis=1,
    )
    merged_projection_weight = (wqkv.astype(jnp.float32) + ADAPTER_SCALE * weight_delta).astype(
        jnp.bfloat16
    )
    output_weight_delta = jnp.dot(
        adapter_down_output,
        adapter_up_whole[:, projection_width:],
        preferred_element_type=jnp.float32,
    )
    merged_output_weight = (wout.astype(jnp.float32) + ADAPTER_SCALE * output_weight_delta).astype(
        jnp.bfloat16
    )
    shard_rows = token_embedding_table.shape[0]
    first_row = (fsdp_index * tensor_count + tensor_index) * shard_rows
    flat_ids = step_token_rows.reshape(-1)
    one_hot = (
        flat_ids[:, None] == first_row + jnp.arange(shard_rows, dtype=jnp.int32)[None, :]
    ).astype(jnp.bfloat16)
    lookup_terms = jnp.dot(one_hot, token_embedding_table, preferred_element_type=jnp.float32)
    looked_up = lax.psum(lookup_terms, ("fsdp", "tensor"))
    embedded = lax.dynamic_slice_in_dim(
        looked_up.reshape(-1, STEPS, model_width), fsdp_index * rows_here, rows_here, 0
    )
    in_rows = wqkv.shape[0]
    cache_keys = key_value_cache[:, :, :key_value_width].reshape(
        rows_here, slots_here, KVH, HEAD_SIZE
    )
    cache_values = key_value_cache[:, :, key_value_width:].reshape(
        rows_here, slots_here, KVH, HEAD_SIZE
    )
    global_slot = tensor_index * slots_here + jnp.arange(slots_here, dtype=jnp.int32)
    visible = global_slot[None, :] < cached_row_lengths[:, None]
    visible_grid = visible[:, None, None, :]

    def own_heads(array):
        return lax.dynamic_slice_in_dim(array, tensor_index * heads_here, heads_here, 1)

    key_list = []
    value_list = []
    results = []
    for decode_step in range(STEPS):
        inputs = embedded[:, decode_step]
        normed = rms_scale(inputs, input_norm_gain.astype(jnp.float32)).astype(jnp.bfloat16)
        normed_slice = lax.dynamic_slice_in_dim(normed, tensor_index * in_rows, in_rows, 1)
        partial_qkv = jnp.dot(
            normed_slice, merged_projection_weight, preferred_element_type=jnp.float32
        )
        projected = lax.psum(partial_qkv, "tensor").astype(jnp.bfloat16)
        queries = (
            projected[:, :query_width]
            .astype(jnp.float32)
            .reshape(rows_here, QUERY_HEADS, HEAD_SIZE)
        )
        new_key = (
            projected[:, query_width : query_width + key_value_width]
            .astype(jnp.float32)
            .reshape(rows_here, KVH, HEAD_SIZE)
        )
        new_value = projected[:, query_width + key_value_width :].reshape(rows_here, KVH, HEAD_SIZE)
        position = (cached_row_lengths + decode_step).astype(jnp.float32)[:, None]
        rotated_query = rotate(rms_scale(queries, query_key_gains[0]), position).astype(
            jnp.bfloat16
        )
        key_list.append(
            rotate(rms_scale(new_key, query_key_gains[1]), position).astype(jnp.bfloat16)
        )
        value_list.append(new_value)
        query_grid = rotated_query.reshape(rows_here, KVH, groups, HEAD_SIZE)
        scores = (
            jnp.einsum(
                "bgrd,bjgd->bgrj", query_grid, cache_keys, preferred_element_type=jnp.float32
            )
            * scaling
        )
        local_max = jnp.max(jnp.where(visible_grid, scores, -1e30), axis=-1)
        weights = jnp.where(visible_grid, jnp.exp(scores - local_max[..., None]), 0.0)
        local_sum = jnp.sum(weights, axis=-1)
        local_acc = jnp.einsum(
            "bgrj,bjgd->bgrd",
            weights.astype(jnp.bfloat16),
            cache_values,
            preferred_element_type=jnp.float32,
        )
        local_max = local_max.reshape(rows_here, QUERY_HEADS)
        local_sum = local_sum.reshape(rows_here, QUERY_HEADS)
        local_acc = local_acc.reshape(rows_here, QUERY_HEADS, HEAD_SIZE)
        merged_parts = combined_all((local_max, local_sum, local_acc), "tensor", fold_parts)
        cache_part = (
            own_heads(merged_parts[0]),
            own_heads(merged_parts[1]),
            own_heads(merged_parts[2]),
        )
        stacked_keys = jnp.stack(key_list, axis=1)
        stacked_values = jnp.stack(value_list, axis=1)
        fresh_scores = (
            jnp.einsum(
                "bgrd,bsgd->bgrs", query_grid, stacked_keys, preferred_element_type=jnp.float32
            )
            * scaling
        )
        fresh_max = jnp.max(fresh_scores, axis=-1)
        fresh_weights = jnp.exp(fresh_scores - fresh_max[..., None])
        fresh_sum = jnp.sum(fresh_weights, axis=-1)
        fresh_acc = jnp.einsum(
            "bgrs,bsgd->bgrd",
            fresh_weights.astype(jnp.bfloat16),
            stacked_values,
            preferred_element_type=jnp.float32,
        )
        fresh_part = (
            own_heads(fresh_max.reshape(rows_here, QUERY_HEADS)),
            own_heads(fresh_sum.reshape(rows_here, QUERY_HEADS)),
            own_heads(fresh_acc.reshape(rows_here, QUERY_HEADS, HEAD_SIZE)),
        )
        combined = fold_parts(cache_part, fresh_part)
        attended = (
            (combined[2] / combined[1][..., None])
            .reshape(rows_here, heads_here * HEAD_SIZE)
            .astype(jnp.bfloat16)
        )
        partial_out = jnp.dot(attended, merged_output_weight, preferred_element_type=jnp.float32)
        summed_out = lax.psum(partial_out, "tensor")
        results.append((inputs + summed_out).astype(jnp.bfloat16))
    return jnp.stack(results, axis=1)


LANES = 128
MESH = pl.DeviceIdType.MESH


def fused_kernel(
    n, chunk,
    rows_ref, length_ref, gain_ref, qk_gain_ref, cos_ref, sin_ref, up_ref,
    wqkv_hbm, wout_hbm, cache_hbm, down_hbm, down_out_hbm,
    out_ref,
    wqkv, wout, cache, down, down_out, up,
    x_recv, x_rows, part_send, part_recv, proj_send, proj_recv, heads, rotated,
    soft_send, soft_recv, out_send, out_recv, final_send,
    load_sem, x_ssem, x_rsem, up_ssem, up_lsem, up_rsem,
    part_ssem, part_rsem, proj_ssem, proj_rsem, soft_ssem, soft_rsem,
    out_ssem, out_rsem, final_ssem, final_rsem,
):
    f = lax.axis_index("fsdp")
    t = lax.axis_index("tensor")
    me = f * n + t
    in_rows = wqkv.shape[0]
    blocks = in_rows // LANES
    width = wqkv.shape[1] // n
    heads_here = width // LANES
    slots = cache.shape[0]
    kv_width = cache.shape[1] // 2
    model_width = in_rows * n
    fine = 32
    q_chunks = width // chunk
    o_chunks = in_rows // chunk
    all_q = n * q_chunks
    f32 = jnp.float32

    loads = [
        pltpu.make_async_copy(down_hbm, down, load_sem.at[0]),
        pltpu.make_async_copy(wqkv_hbm, wqkv, load_sem.at[1]),
        pltpu.make_async_copy(cache_hbm.at[0], cache, load_sem.at[2]),
        pltpu.make_async_copy(wout_hbm, wout, load_sem.at[3]),
        pltpu.make_async_copy(down_out_hbm, down_out, load_sem.at[4]),
    ]
    for load in loads:
        load.start()

    barrier = pltpu.get_barrier_semaphore()

    @pl.loop(1, 2 * n)
    def _(i):
        peer = lax.rem(me + i, 2 * n)
        pl.semaphore_signal(
            barrier, inc=1, device_id={"fsdp": peer // n, "tensor": lax.rem(peer, n)},
            device_id_type=MESH,
        )

    pl.semaphore_wait(barrier, 2 * n - 1)

    def x_copy(peer, slot):
        return pltpu.make_async_remote_copy(
            src_ref=rows_ref.at[peer], dst_ref=x_recv.at[slot],
            send_sem=x_ssem.at[peer], recv_sem=x_rsem.at[slot],
            device_id={"fsdp": peer // n, "tensor": lax.rem(peer, n)}, device_id_type=MESH,
        )

    @pl.loop(1, 2 * n)
    def _(i):
        peer = lax.rem(me + i, 2 * n)
        x_copy(peer, me).start()

    pieces = up_ref.shape[0]

    def up_route(c):
        g = pieces * me + c
        for_q = g < all_q
        target = jnp.where(for_q, g // q_chunks, (g - all_q) // o_chunks)
        slot = jnp.where(for_q, lax.rem(g, q_chunks), q_chunks + lax.rem(g, o_chunks))
        return target, slot

    def up_copy(c, fd):
        target, slot = up_route(c)
        return pltpu.make_async_remote_copy(
            src_ref=up_ref.at[c], dst_ref=up.at[slot],
            send_sem=up_ssem.at[c, fd], recv_sem=up_rsem.at[slot],
            device_id={"fsdp": fd, "tensor": target}, device_id_type=MESH,
        )

    for c in range(pieces):
        for fd in range(2):
            target, slot = up_route(c)
            same = jnp.logical_and(target == t, f == fd)

            @pl.when(same)
            def _():
                pltpu.make_async_copy(up_ref.at[c], up.at[slot], up_rsem.at[slot]).start()

            @pl.when(jnp.logical_not(same))
            def _():
                up_copy(c, fd).start()

    def peers_copy(src, dst, ssem, rsem, target, slot):
        return pltpu.make_async_remote_copy(
            src_ref=src, dst_ref=dst, send_sem=ssem.at[target], recv_sem=rsem.at[slot],
            device_id={"fsdp": f, "tensor": target}, device_id_type=MESH,
        )

    x_rows[...] = rows_ref[me].astype(f32)

    @pl.loop(1, 2 * n)
    def _(i):
        peer = lax.rem(me + i, 2 * n)
        x_copy(peer, peer).wait_recv()
        x_rows[...] += x_recv[peer].astype(f32)

    def flat(values, count):
        return jnp.concatenate(
            [values[STEPS * j : STEPS * (j + 1)] for j in range(count)], axis=1
        )

    def tall(values, count):
        return jnp.concatenate(
            [values[:STEPS, LANES * j : LANES * (j + 1)] for j in range(count)], axis=0
        )

    def nt(a, b):
        return lax.dot_general(a, b, (((1,), (1,)), ((), ())), preferred_element_type=f32)

    def nt_fine(a, b):
        high = a.astype(jnp.bfloat16)
        low = (a - high.astype(f32)).astype(jnp.bfloat16)
        return nt(high, b) + nt(low, b)

    x = flat(x_rows[...], blocks)
    gain = gain_ref[:, pl.ds(pl.multiple_of(t * in_rows, LANES), in_rows)].astype(f32)
    scaled = (x * gain).astype(jnp.bfloat16)
    square = jnp.broadcast_to(jnp.sum(x * x, axis=1, keepdims=True), (STEPS, LANES))
    loads[0].wait()
    low = jnp.dot(scaled, down[...], preferred_element_type=f32)
    extra = jnp.concatenate([tall(low, 3), square], axis=0)
    loads[1].wait()

    @pl.loop(0, n)
    def _(i):
        target = lax.rem(t + 1 + i, n)
        part = jnp.dot(
            scaled, wqkv[:, pl.ds(pl.multiple_of(target * width, LANES), width)],
            preferred_element_type=f32,
        )
        part_send[target] = jnp.concatenate([tall(part, heads_here), extra], axis=0)

        @pl.when(i < n - 1)
        def _():
            peers_copy(
                part_send.at[target], part_recv.at[t], part_ssem, part_rsem, target, t
            ).start()

    for slot in range(q_chunks):
        pltpu.make_async_copy(up_ref.at[0], up.at[slot], up_rsem.at[slot]).wait()
    total = part_send[t]
    for i in range(1, n):
        source = lax.rem(t + i, n)
        peers_copy(
            part_send.at[source], part_recv.at[source], part_ssem, part_rsem, source, source
        ).wait_recv()
        total = total + part_recv[source]
    base = STEPS * heads_here
    rate = lax.rsqrt(total[base + 3 * STEPS :] * (1.0 / model_width) + EPSILON)
    factors = total[base : base + 3 * STEPS]
    delta = nt_fine(factors, up[:q_chunks].reshape(width, LANES))
    pieces_out = []
    for j in range(heads_here):
        head = t * heads_here + j
        mine = delta[:, LANES * j : LANES * (j + 1)]
        picked = jnp.where(
            head < QUERY_HEADS,
            mine[:STEPS],
            jnp.where(head < QUERY_HEADS + KVH, mine[STEPS : 2 * STEPS], mine[2 * STEPS :]),
        )
        pieces_out.append((total[STEPS * j : STEPS * (j + 1)] + ADAPTER_SCALE * picked) * rate)
    spare = proj_send.shape[0] - base
    pieces_out.append(jnp.zeros((spare, LANES), f32))
    proj_send[...] = jnp.concatenate(pieces_out, axis=0).astype(jnp.bfloat16)

    @pl.loop(1, n)
    def _(i):
        target = lax.rem(t + i, n)
        peers_copy(proj_send, proj_recv.at[t], proj_ssem, proj_rsem, target, t).start()

    heads[t] = proj_send[...].astype(f32)[:base]

    @pl.loop(1, n)
    def _(i):
        source = lax.rem(t + i, n)
        peers_copy(
            proj_send, proj_recv.at[source], proj_ssem, proj_rsem, source, source
        ).wait_recv()
        heads[source] = proj_recv[source].astype(f32)[:base]

    every = heads[...].reshape(n * base, LANES)
    q_rows = STEPS * QUERY_HEADS
    k_rows = STEPS * KVH

    def turned(values, scale):
        count = values.shape[0]
        ms = jnp.mean(values * values, axis=1, keepdims=True)
        values = values * lax.rsqrt(ms + EPSILON) * scale
        cosine = jnp.concatenate([cos_ref[...]] * (count // 8), axis=0)
        sine = jnp.concatenate([sin_ref[...]] * (count // 8), axis=0)
        return (values * cosine + pltpu.roll(values, LANES // 2, 1) * sine).astype(jnp.bfloat16)

    rotated[...] = turned(every[:q_rows], qk_gain_ref[0:1, :])
    new_keys = turned(every[q_rows : q_rows + k_rows], qk_gain_ref[1:2, :])
    new_values = every[q_rows + k_rows :].astype(jnp.bfloat16)

    scaling = 1.0 / math.sqrt(HEAD_SIZE)
    length = length_ref[0]
    loads[2].wait()
    place = t * slots + lax.broadcasted_iota(jnp.int32, (1, slots), 1)
    visible = place < length
    diagonal = lax.broadcasted_iota(jnp.int32, (fine, LANES), 0) == lax.broadcasted_iota(
        jnp.int32, (fine, LANES), 1
    )
    top_row = lax.broadcasted_iota(jnp.int32, (8, LANES), 0) == 0

    def to_row(column):
        return jnp.sum(jnp.where(diagonal, column, 0.0), axis=0, keepdims=True)

    def to_column(row):
        return jnp.sum(jnp.where(diagonal, row, 0.0), axis=1, keepdims=True)

    @pl.loop(0, n)
    def _(i):
        g = lax.rem(t + 1 + i, n)
        query = rotated[pl.ds(pl.multiple_of(g * fine, fine), fine)]
        keys = cache[:, pl.ds(pl.multiple_of(g * LANES, LANES), LANES)]
        values = cache[:, pl.ds(pl.multiple_of(kv_width + g * LANES, LANES), LANES)]
        scores = jnp.where(visible, nt(query, keys) * scaling, -1e30)
        top = jnp.max(scores, axis=1, keepdims=True)
        weights = jnp.where(visible, jnp.exp(scores - top), 0.0)
        count = jnp.sum(weights, axis=1, keepdims=True)
        soft_send[g, :fine] = jnp.dot(
            weights.astype(jnp.bfloat16), values, preferred_element_type=f32
        )
        soft_send[g, fine:] = jnp.where(top_row, to_row(top), to_row(count))

        @pl.when(i < n - 1)
        def _():
            peers_copy(soft_send.at[g], soft_recv.at[t], soft_ssem, soft_rsem, g, t).start()

    own = rotated[pl.ds(pl.multiple_of(t * fine, fine), fine)]
    fresh = nt(own, new_keys) * scaling
    row = lax.broadcasted_iota(jnp.int32, (fine, k_rows), 0)
    col = lax.broadcasted_iota(jnp.int32, (fine, k_rows), 1)
    allowed = jnp.logical_and(col // STEPS == t, col % STEPS <= row % STEPS)
    fresh = jnp.where(allowed, fresh, -1e30)
    fresh_top = jnp.max(fresh, axis=1, keepdims=True)

    soft_recv[t] = soft_send[t]
    for i in range(1, n):
        source = lax.rem(t + i, n)
        peers_copy(
            soft_send.at[source], soft_recv.at[source], soft_ssem, soft_rsem, source, source
        ).wait_recv()
    tops = [to_column(soft_recv[i, fine : fine + 1]) for i in range(n)]
    largest = fresh_top
    for top in tops:
        largest = jnp.maximum(largest, top)
    weights = jnp.where(allowed, jnp.exp(fresh - largest), 0.0)
    denominator = jnp.sum(weights, axis=1, keepdims=True)
    numerator = jnp.dot(weights.astype(jnp.bfloat16), new_values, preferred_element_type=f32)
    for i in range(n):
        factor = jnp.exp(tops[i] - largest)
        denominator += factor * to_column(soft_recv[i, fine + 1 : fine + 2])
        numerator += factor * soft_recv[i, :fine]
    attended = flat(numerator / denominator, fine // STEPS).astype(jnp.bfloat16)

    loads[3].wait()
    loads[4].wait()
    low_out = jnp.dot(attended, down_out[...], preferred_element_type=f32)

    @pl.loop(0, n)
    def _(i):
        target = lax.rem(t + 1 + i, n)
        part = jnp.dot(
            attended, wout[:, pl.ds(pl.multiple_of(target * in_rows, LANES), in_rows)],
            preferred_element_type=f32,
        )
        out_send[target] = jnp.concatenate([tall(part, blocks), low_out], axis=0)

        @pl.when(i < n - 1)
        def _():
            peers_copy(
                out_send.at[target], out_recv.at[t], out_ssem, out_rsem, target, t
            ).start()

    for slot in range(q_chunks, q_chunks + o_chunks):
        pltpu.make_async_copy(up_ref.at[0], up.at[slot], up_rsem.at[slot]).wait()
    summed = out_send[t]
    for i in range(1, n):
        source = lax.rem(t + i, n)
        peers_copy(
            out_send.at[source], out_recv.at[source], out_ssem, out_rsem, source, source
        ).wait_recv()
        summed = summed + out_recv[source]
    base_out = STEPS * blocks
    delta_out = tall(
        nt_fine(summed[base_out:], up[q_chunks:].reshape(in_rows, LANES)), blocks
    )
    hidden = x_rows[:base_out] + summed[:base_out] + ADAPTER_SCALE * delta_out
    spare_out = final_send.shape[0] - base_out
    final_send[...] = jnp.concatenate(
        [hidden, jnp.zeros((spare_out, LANES), f32)], axis=0
    ).astype(jnp.bfloat16)

    @pl.loop(1, n)
    def _(i):
        target = lax.rem(t + i, n)
        peers_copy(final_send, out_ref.at[t], final_ssem, final_rsem, target, t).start()

    out_ref[t] = final_send[...]

    @pl.loop(1, n)
    def _(i):
        source = lax.rem(t + i, n)
        peers_copy(
            final_send, out_ref.at[source], final_ssem, final_rsem, source, source
        ).wait_recv()

    @pl.loop(1, 2 * n)
    def _(i):
        peer = lax.rem(me + i, 2 * n)
        x_copy(peer, me).wait_send()

    for c in range(pieces):
        for fd in range(2):
            target, slot = up_route(c)

            @pl.when(jnp.logical_not(jnp.logical_and(target == t, f == fd)))
            def _():
                up_copy(c, fd).wait_send()

    @pl.loop(1, n)
    def _(i):
        target = lax.rem(t + i, n)
        peers_copy(
            part_send.at[target], part_recv.at[t], part_ssem, part_rsem, target, t
        ).wait_send()
        peers_copy(proj_send, proj_recv.at[t], proj_ssem, proj_rsem, target, t).wait_send()
        peers_copy(
            soft_send.at[target], soft_recv.at[t], soft_ssem, soft_rsem, target, t
        ).wait_send()
        peers_copy(
            out_send.at[target], out_recv.at[t], out_ssem, out_rsem, target, t
        ).wait_send()
        peers_copy(final_send, out_ref.at[t], final_ssem, final_rsem, target, t).wait_send()


def up_to(count, multiple):
    return -(-count // multiple) * multiple


def fused(
    step_token_rows,
    token_embedding_table,
    cached_row_lengths,
    key_value_cache,
    input_norm_gain,
    query_key_gains,
    wqkv,
    wout,
    adapter_down_projections,
    adapter_down_output,
    adapter_up_factors,
):
    n = lax.axis_size("tensor")
    f = lax.axis_index("fsdp")
    t = lax.axis_index("tensor")
    in_rows, projection_width = wqkv.shape
    model_width = wout.shape[1]
    width = projection_width // n
    shard_rows = token_embedding_table.shape[0]
    shard = adapter_up_factors.shape[1]
    chunk = math.gcd(math.gcd(shard, width), in_rows)
    pieces = shard // chunk
    blocks = in_rows // LANES
    heads_here = width // LANES
    bf16, f32 = jnp.bfloat16, jnp.float32

    local_ids = step_token_rows.reshape(-1) - (f * n + t) * shard_rows
    held = jnp.logical_and(local_ids >= 0, local_ids < shard_rows)
    rows = jnp.where(
        held[:, None], token_embedding_table[jnp.clip(local_ids, 0, shard_rows - 1)], 0
    ).astype(bf16)
    rows = rows.reshape(2, STEPS, n, blocks, LANES).transpose(0, 2, 3, 1, 4)
    rows = rows.reshape(2 * n, STEPS * blocks, LANES)
    x_tall = up_to(STEPS * blocks, 16)
    rows = jnp.pad(rows, ((0, 0), (0, x_tall - STEPS * blocks), (0, 0)))

    half = HEAD_SIZE // 2
    inverse = ROPE_BASE ** (-(2.0 * jnp.arange(half, dtype=f32)) / HEAD_SIZE)
    position = (cached_row_lengths[0] + jnp.arange(8, dtype=jnp.int32) % STEPS).astype(f32)
    angle = position[:, None] * inverse
    cosine = jnp.cos(angle)
    sine = jnp.sin(angle)
    cosine = jnp.concatenate([cosine, cosine], axis=1)
    sine = jnp.concatenate([-sine, sine], axis=1)
    up = adapter_up_factors.T.reshape(pieces, chunk, LANES)

    part_rows = STEPS * (heads_here + 4)
    proj_rows = up_to(STEPS * heads_here, 16)
    soft_rows = 32 + 8
    out_rows = STEPS * (blocks + 1)
    slots_up = (width + in_rows) // chunk
    vmem = pl.BlockSpec(memory_space=pltpu.VMEM)
    smem = pl.BlockSpec(memory_space=pltpu.SMEM)
    hbm = pl.BlockSpec(memory_space=pl.ANY)
    dma = pltpu.SemaphoreType.DMA
    result = pl.pallas_call(
        lambda *refs: fused_kernel(n, chunk, *refs),
        out_shape=jax.ShapeDtypeStruct((n, x_tall, LANES), bf16),
        in_specs=[vmem, smem, vmem, vmem, vmem, vmem, vmem] + [hbm] * 5,
        out_specs=vmem,
        scratch_shapes=[
            pltpu.VMEM(wqkv.shape, bf16),
            pltpu.VMEM(wout.shape, bf16),
            pltpu.VMEM(key_value_cache.shape[1:], bf16),
            pltpu.VMEM(adapter_down_projections.shape, bf16),
            pltpu.VMEM(adapter_down_output.shape, bf16),
            pltpu.VMEM((slots_up, chunk, LANES), bf16),
            pltpu.VMEM((2 * n, x_tall, LANES), bf16),
            pltpu.VMEM((x_tall, LANES), f32),
            pltpu.VMEM((n, part_rows, LANES), f32),
            pltpu.VMEM((n, part_rows, LANES), f32),
            pltpu.VMEM((proj_rows, LANES), bf16),
            pltpu.VMEM((n, proj_rows, LANES), bf16),
            pltpu.VMEM((n, STEPS * heads_here, LANES), f32),
            pltpu.VMEM((STEPS * QUERY_HEADS, LANES), bf16),
            pltpu.VMEM((n, soft_rows, LANES), f32),
            pltpu.VMEM((n, soft_rows, LANES), f32),
            pltpu.VMEM((n, out_rows, LANES), f32),
            pltpu.VMEM((n, out_rows, LANES), f32),
            pltpu.VMEM((x_tall, LANES), bf16),
            dma((5,)),
            dma((2 * n,)),
            dma((2 * n,)),
            dma((pieces, 2)),
            dma((slots_up,)),
            dma((slots_up,)),
        ]
        + [dma((n,))] * 10,
        compiler_params=pltpu.CompilerParams(
            collective_id=0, has_side_effects=True, vmem_limit_bytes=52 * 1024 * 1024
        ),
    )(
        rows,
        cached_row_lengths,
        input_norm_gain.reshape(1, model_width),
        query_key_gains,
        cosine,
        sine,
        up,
        wqkv,
        wout,
        key_value_cache,
        adapter_down_projections,
        adapter_down_output,
    )
    result = result[:, : STEPS * blocks].reshape(n, blocks, STEPS, LANES)
    return result.transpose(2, 0, 1, 3).reshape(1, STEPS, model_width)


def solution(mesh):
    in_specs = (
        P("group", None),
        P(("fsdp", "tensor"), None),
        P(("group", "fsdp")),
        P(("group", "fsdp"), "tensor", None),
        P(),
        P(),
        P("tensor", None),
        P("tensor", None),
        P("tensor", None),
        P("tensor", None),
        P(None, ("fsdp", "tensor")),
    )
    out_specs = P(("group", "fsdp"), None, None)
    fits = (
        mesh.shape["tensor"] == KVH
        and mesh.shape["fsdp"] == 2
        and HEAD_SIZE == LANES
        and ADAPTER_RANK == LANES
    )
    body = fused if fits else local
    return jax.shard_map(body, mesh=mesh, in_specs=in_specs, out_specs=out_specs, check_vma=False)
```

```python
import math

import jax
import jax.numpy as jnp
from jax import lax
from jax.experimental import pallas as pl
from jax.experimental.pallas import tpu as pltpu
from jax.sharding import PartitionSpec as P

QUERY_HEADS = 64
KVH = 8
HEAD_SIZE = 128
ADAPTER_RANK = 128
STEPS = 4


EPSILON = 1e-06
ROPE_BASE = 1000000.0
ADAPTER_SCALE = 2.0


def combined_all(x, axis, join):
    gathered = jax.tree.map(
        lambda a, kind: lax.all_gather(a.astype(kind), axis),
        x,
        (jnp.bfloat16, jnp.bfloat16, jnp.bfloat16),
    )

    def take(source):
        return jax.tree.map(
            lambda a, own: lax.dynamic_index_in_dim(a, source, 0, False).astype(own.dtype),
            gathered,
            x,
        )

    return lax.fori_loop(
        1, lax.axis_size(axis), lambda source, state: join(state, take(source)), take(0)
    )


def rms_scale(values, gain):
    return values * lax.rsqrt(jnp.mean(values * values, axis=-1, keepdims=True) + EPSILON) * gain


def rotate(values, position):
    half_width = values.shape[-1] // 2
    inverse = ROPE_BASE ** (-(2.0 * jnp.arange(half_width, dtype=jnp.float32)) / values.shape[-1])
    angle = position[..., None] * inverse
    cosine = jnp.cos(angle)
    sine = jnp.sin(angle)
    first_half = values[..., :half_width]
    second_half = values[..., half_width:]
    return jnp.concatenate(
        [first_half * cosine - second_half * sine, second_half * cosine + first_half * sine],
        axis=-1,
    )


def fold_parts(earlier, later):
    top = jnp.maximum(earlier[0], later[0])
    scale_one = jnp.exp(earlier[0] - top)
    scale_two = jnp.exp(later[0] - top)
    return (
        top,
        earlier[1] * scale_one + later[1] * scale_two,
        earlier[2] * scale_one[..., None] + later[2] * scale_two[..., None],
    )


def local(
    step_token_rows,
    token_embedding_table,
    cached_row_lengths,
    key_value_cache,
    input_norm_gain,
    query_key_gains,
    wqkv,
    wout,
    adapter_down_projections,
    adapter_down_output,
    adapter_up_factors,
):
    tensor_count = lax.axis_size("tensor")
    tensor_index = lax.axis_index("tensor")
    fsdp_index = lax.axis_index("fsdp")
    rows_here = cached_row_lengths.shape[0]
    heads_here = QUERY_HEADS // tensor_count
    slots_here = key_value_cache.shape[1]
    groups = QUERY_HEADS // KVH
    query_width = QUERY_HEADS * HEAD_SIZE
    key_value_width = KVH * HEAD_SIZE
    projection_width = wqkv.shape[1]
    model_width = token_embedding_table.shape[1]
    scaling = 1.0 / math.sqrt(HEAD_SIZE)
    adapter_up_whole = lax.all_gather(adapter_up_factors, ("fsdp", "tensor"), axis=1, tiled=True)
    weight_delta = jnp.concatenate(
        [
            jnp.dot(
                adapter_down_projections[:, :ADAPTER_RANK],
                adapter_up_whole[:, :query_width],
                preferred_element_type=jnp.float32,
            ),
            jnp.dot(
                adapter_down_projections[:, ADAPTER_RANK : 2 * ADAPTER_RANK],
                adapter_up_whole[:, query_width : query_width + key_value_width],
                preferred_element_type=jnp.float32,
            ),
            jnp.dot(
                adapter_down_projections[:, 2 * ADAPTER_RANK :],
                adapter_up_whole[:, query_width + key_value_width : projection_width],
                preferred_element_type=jnp.float32,
            ),
        ],
        axis=1,
    )
    merged_projection_weight = (wqkv.astype(jnp.float32) + ADAPTER_SCALE * weight_delta).astype(
        jnp.bfloat16
    )
    output_weight_delta = jnp.dot(
        adapter_down_output,
        adapter_up_whole[:, projection_width:],
        preferred_element_type=jnp.float32,
    )
    merged_output_weight = (wout.astype(jnp.float32) + ADAPTER_SCALE * output_weight_delta).astype(
        jnp.bfloat16
    )
    shard_rows = token_embedding_table.shape[0]
    first_row = (fsdp_index * tensor_count + tensor_index) * shard_rows
    flat_ids = step_token_rows.reshape(-1)
    one_hot = (
        flat_ids[:, None] == first_row + jnp.arange(shard_rows, dtype=jnp.int32)[None, :]
    ).astype(jnp.bfloat16)
    lookup_terms = jnp.dot(one_hot, token_embedding_table, preferred_element_type=jnp.float32)
    looked_up = lax.psum(lookup_terms, ("fsdp", "tensor"))
    embedded = lax.dynamic_slice_in_dim(
        looked_up.reshape(-1, STEPS, model_width), fsdp_index * rows_here, rows_here, 0
    )
    in_rows = wqkv.shape[0]
    cache_keys = key_value_cache[:, :, :key_value_width].reshape(
        rows_here, slots_here, KVH, HEAD_SIZE
    )
    cache_values = key_value_cache[:, :, key_value_width:].reshape(
        rows_here, slots_here, KVH, HEAD_SIZE
    )
    global_slot = tensor_index * slots_here + jnp.arange(slots_here, dtype=jnp.int32)
    visible = global_slot[None, :] < cached_row_lengths[:, None]
    visible_grid = visible[:, None, None, :]

    def own_heads(array):
        return lax.dynamic_slice_in_dim(array, tensor_index * heads_here, heads_here, 1)

    key_list = []
    value_list = []
    results = []
    for decode_step in range(STEPS):
        inputs = embedded[:, decode_step]
        normed = rms_scale(inputs, input_norm_gain.astype(jnp.float32)).astype(jnp.bfloat16)
        normed_slice = lax.dynamic_slice_in_dim(normed, tensor_index * in_rows, in_rows, 1)
        partial_qkv = jnp.dot(
            normed_slice, merged_projection_weight, preferred_element_type=jnp.float32
        )
        projected = lax.psum(partial_qkv, "tensor").astype(jnp.bfloat16)
        queries = (
            projected[:, :query_width]
            .astype(jnp.float32)
            .reshape(rows_here, QUERY_HEADS, HEAD_SIZE)
        )
        new_key = (
            projected[:, query_width : query_width + key_value_width]
            .astype(jnp.float32)
            .reshape(rows_here, KVH, HEAD_SIZE)
        )
        new_value = projected[:, query_width + key_value_width :].reshape(rows_here, KVH, HEAD_SIZE)
        position = (cached_row_lengths + decode_step).astype(jnp.float32)[:, None]
        rotated_query = rotate(rms_scale(queries, query_key_gains[0]), position).astype(
            jnp.bfloat16
        )
        key_list.append(
            rotate(rms_scale(new_key, query_key_gains[1]), position).astype(jnp.bfloat16)
        )
        value_list.append(new_value)
        query_grid = rotated_query.reshape(rows_here, KVH, groups, HEAD_SIZE)
        scores = (
            jnp.einsum(
                "bgrd,bjgd->bgrj", query_grid, cache_keys, preferred_element_type=jnp.float32
            )
            * scaling
        )
        local_max = jnp.max(jnp.where(visible_grid, scores, -1e30), axis=-1)
        weights = jnp.where(visible_grid, jnp.exp(scores - local_max[..., None]), 0.0)
        local_sum = jnp.sum(weights, axis=-1)
        local_acc = jnp.einsum(
            "bgrj,bjgd->bgrd",
            weights.astype(jnp.bfloat16),
            cache_values,
            preferred_element_type=jnp.float32,
        )
        local_max = local_max.reshape(rows_here, QUERY_HEADS)
        local_sum = local_sum.reshape(rows_here, QUERY_HEADS)
        local_acc = local_acc.reshape(rows_here, QUERY_HEADS, HEAD_SIZE)
        merged_parts = combined_all((local_max, local_sum, local_acc), "tensor", fold_parts)
        cache_part = (
            own_heads(merged_parts[0]),
            own_heads(merged_parts[1]),
            own_heads(merged_parts[2]),
        )
        stacked_keys = jnp.stack(key_list, axis=1)
        stacked_values = jnp.stack(value_list, axis=1)
        fresh_scores = (
            jnp.einsum(
                "bgrd,bsgd->bgrs", query_grid, stacked_keys, preferred_element_type=jnp.float32
            )
            * scaling
        )
        fresh_max = jnp.max(fresh_scores, axis=-1)
        fresh_weights = jnp.exp(fresh_scores - fresh_max[..., None])
        fresh_sum = jnp.sum(fresh_weights, axis=-1)
        fresh_acc = jnp.einsum(
            "bgrs,bsgd->bgrd",
            fresh_weights.astype(jnp.bfloat16),
            stacked_values,
            preferred_element_type=jnp.float32,
        )
        fresh_part = (
            own_heads(fresh_max.reshape(rows_here, QUERY_HEADS)),
            own_heads(fresh_sum.reshape(rows_here, QUERY_HEADS)),
            own_heads(fresh_acc.reshape(rows_here, QUERY_HEADS, HEAD_SIZE)),
        )
        combined = fold_parts(cache_part, fresh_part)
        attended = (
            (combined[2] / combined[1][..., None])
            .reshape(rows_here, heads_here * HEAD_SIZE)
            .astype(jnp.bfloat16)
        )
        partial_out = jnp.dot(attended, merged_output_weight, preferred_element_type=jnp.float32)
        summed_out = lax.psum(partial_out, "tensor")
        results.append((inputs + summed_out).astype(jnp.bfloat16))
    return jnp.stack(results, axis=1)


LANES = 128
MESH = pl.DeviceIdType.MESH


def fused_kernel(
    n, chunk,
    ids_ref, length_ref, gain_ref, cos_ref, sin_ref, qk_gain_hbm, up_ref, table_hbm,
    wqkv_hbm, wout_hbm, cache_hbm, down_hbm, down_out_hbm,
    out_ref,
    table, wqkv, wout, cache, down, down_out, qk_gain_ref, up, x_send,
    x_recv, x_rows, part_send, part_recv, proj_send, proj_recv, heads, rotated,
    soft_send, soft_recv, out_send, out_recv, final_send,
    load_sem, x_ssem, x_rsem, up_ssem, up_lsem, up_rsem,
    part_ssem, part_rsem, proj_ssem, proj_rsem, soft_ssem, soft_rsem,
    out_ssem, out_rsem, final_ssem, final_rsem,
):
    f = lax.axis_index("fsdp")
    t = lax.axis_index("tensor")
    me = f * n + t
    in_rows = wqkv.shape[0]
    blocks = in_rows // LANES
    width = wqkv.shape[1] // n
    heads_here = width // LANES
    slots = cache.shape[0]
    kv_width = cache.shape[1] // 2
    model_width = in_rows * n
    fine = 32
    q_chunks = width // chunk
    o_chunks = in_rows // chunk
    all_q = n * q_chunks
    f32 = jnp.float32

    loads = [
        pltpu.make_async_copy(table_hbm, table, load_sem.at[5]),
        pltpu.make_async_copy(qk_gain_hbm, qk_gain_ref, load_sem.at[6]),
        pltpu.make_async_copy(down_hbm, down, load_sem.at[0]),
        pltpu.make_async_copy(wqkv_hbm, wqkv, load_sem.at[1]),
        pltpu.make_async_copy(cache_hbm.at[0], cache, load_sem.at[2]),
        pltpu.make_async_copy(wout_hbm, wout, load_sem.at[3]),
        pltpu.make_async_copy(down_out_hbm, down_out, load_sem.at[4]),
    ]
    for load in loads:
        load.start()

    barrier = pltpu.get_barrier_semaphore()

    @pl.loop(1, 2 * n)
    def _(i):
        peer = lax.rem(me + i, 2 * n)
        pl.semaphore_signal(
            barrier, inc=1, device_id={"fsdp": peer // n, "tensor": lax.rem(peer, n)},
            device_id_type=MESH,
        )

    pl.semaphore_wait(barrier, 2 * n - 1)

    def x_copy(peer, slot):
        return pltpu.make_async_remote_copy(
            src_ref=x_send.at[peer], dst_ref=x_recv.at[slot],
            send_sem=x_ssem.at[peer], recv_sem=x_rsem.at[slot],
            device_id={"fsdp": peer // n, "tensor": lax.rem(peer, n)}, device_id_type=MESH,
        )

    shard_rows = table.shape[0]
    tokens = lax.broadcasted_iota(jnp.int32, (2 * STEPS, shard_rows), 0)
    local_row = lax.broadcasted_iota(jnp.int32, (2 * STEPS, shard_rows), 1) + me * shard_rows
    wanted = jnp.zeros((2 * STEPS, shard_rows), jnp.int32)
    for k in range(2 * STEPS):
        wanted = jnp.where(tokens == k, ids_ref[k // STEPS, k % STEPS], wanted)
    one_hot = jnp.where(wanted == local_row, 1.0, 0.0).astype(jnp.bfloat16)
    x_pad = jnp.zeros((x_rows.shape[0] - STEPS * blocks, LANES), f32)
    loads[0].wait()

    @pl.loop(0, n)
    def _(i):
        target = lax.rem(t + 1 + i, n)
        found = jnp.dot(
            one_hot, table[:, pl.ds(pl.multiple_of(target * in_rows, LANES), in_rows)],
            preferred_element_type=f32,
        )
        for fd in range(2):
            mine = jnp.concatenate(
                [
                    found[STEPS * fd : STEPS * (fd + 1), LANES * j : LANES * (j + 1)]
                    for j in range(blocks)
                ]
                + [x_pad],
                axis=0,
            )
            peer = fd * n + target
            x_send[peer] = mine.astype(jnp.bfloat16)

            @pl.when(peer != me)
            def _():
                x_copy(peer, me).start()

    pieces = up_ref.shape[0]

    def up_route(c):
        g = pieces * me + c
        for_q = g < all_q
        target = jnp.where(for_q, g // q_chunks, (g - all_q) // o_chunks)
        slot = jnp.where(for_q, lax.rem(g, q_chunks), q_chunks + lax.rem(g, o_chunks))
        return target, slot

    def up_copy(c, fd):
        target, slot = up_route(c)
        return pltpu.make_async_remote_copy(
            src_ref=up_ref.at[c], dst_ref=up.at[slot],
            send_sem=up_ssem.at[c, fd], recv_sem=up_rsem.at[slot],
            device_id={"fsdp": fd, "tensor": target}, device_id_type=MESH,
        )

    for c in range(pieces):
        for fd in range(2):
            target, slot = up_route(c)
            same = jnp.logical_and(target == t, f == fd)

            @pl.when(same)
            def _():
                pltpu.make_async_copy(up_ref.at[c], up.at[slot], up_rsem.at[slot]).start()

            @pl.when(jnp.logical_not(same))
            def _():
                up_copy(c, fd).start()

    def peers_copy(src, dst, ssem, rsem, target, slot):
        return pltpu.make_async_remote_copy(
            src_ref=src, dst_ref=dst, send_sem=ssem.at[target], recv_sem=rsem.at[slot],
            device_id={"fsdp": f, "tensor": target}, device_id_type=MESH,
        )

    x_rows[...] = x_send[me].astype(f32)

    @pl.loop(1, 2 * n)
    def _(i):
        peer = lax.rem(me + i, 2 * n)
        x_copy(peer, peer).wait_recv()
        x_rows[...] += x_recv[peer].astype(f32)

    def flat(values, count):
        return jnp.concatenate(
            [values[STEPS * j : STEPS * (j + 1)] for j in range(count)], axis=1
        )

    def tall(values, count):
        return jnp.concatenate(
            [values[:STEPS, LANES * j : LANES * (j + 1)] for j in range(count)], axis=0
        )

    def nt(a, b):
        return lax.dot_general(a, b, (((1,), (1,)), ((), ())), preferred_element_type=f32)

    def nt_fine(a, b):
        high = a.astype(jnp.bfloat16)
        low = (a - high.astype(f32)).astype(jnp.bfloat16)
        return nt(high, b) + nt(low, b)

    x = flat(x_rows[...], blocks)
    gain = gain_ref[:, pl.ds(pl.multiple_of(t * in_rows, LANES), in_rows)].astype(f32)
    scaled = (x * gain).astype(jnp.bfloat16)
    square = jnp.broadcast_to(jnp.sum(x * x, axis=1, keepdims=True), (STEPS, LANES))
    loads[2].wait()
    low = jnp.dot(scaled, down[...], preferred_element_type=f32)
    extra = jnp.concatenate([tall(low, 3), square], axis=0)
    loads[3].wait()

    @pl.loop(0, n)
    def _(i):
        target = lax.rem(t + 1 + i, n)
        part = jnp.dot(
            scaled, wqkv[:, pl.ds(pl.multiple_of(target * width, LANES), width)],
            preferred_element_type=f32,
        )
        part_send[target] = jnp.concatenate([tall(part, heads_here), extra], axis=0)

        @pl.when(i < n - 1)
        def _():
            peers_copy(
                part_send.at[target], part_recv.at[t], part_ssem, part_rsem, target, t
            ).start()

    for slot in range(q_chunks):
        pltpu.make_async_copy(up_ref.at[0], up.at[slot], up_rsem.at[slot]).wait()
    total = part_send[t]
    for i in range(1, n):
        source = lax.rem(t + i, n)
        peers_copy(
            part_send.at[source], part_recv.at[source], part_ssem, part_rsem, source, source
        ).wait_recv()
        total = total + part_recv[source]
    base = STEPS * heads_here
    rate = lax.rsqrt(total[base + 3 * STEPS :] * (1.0 / model_width) + EPSILON)
    factors = total[base : base + 3 * STEPS]
    delta = nt_fine(factors, up[:q_chunks].reshape(width, LANES))
    pieces_out = []
    for j in range(heads_here):
        head = t * heads_here + j
        mine = delta[:, LANES * j : LANES * (j + 1)]
        picked = jnp.where(
            head < QUERY_HEADS,
            mine[:STEPS],
            jnp.where(head < QUERY_HEADS + KVH, mine[STEPS : 2 * STEPS], mine[2 * STEPS :]),
        )
        pieces_out.append((total[STEPS * j : STEPS * (j + 1)] + ADAPTER_SCALE * picked) * rate)
    spare = proj_send.shape[0] - base
    pieces_out.append(jnp.zeros((spare, LANES), f32))
    proj_send[...] = jnp.concatenate(pieces_out, axis=0).astype(jnp.bfloat16)

    @pl.loop(1, n)
    def _(i):
        target = lax.rem(t + i, n)
        peers_copy(proj_send, proj_recv.at[t], proj_ssem, proj_rsem, target, t).start()

    heads[t] = proj_send[...].astype(f32)[:base]

    @pl.loop(1, n)
    def _(i):
        source = lax.rem(t + i, n)
        peers_copy(
            proj_send, proj_recv.at[source], proj_ssem, proj_rsem, source, source
        ).wait_recv()
        heads[source] = proj_recv[source].astype(f32)[:base]

    every = heads[...].reshape(n * base, LANES)
    q_rows = STEPS * QUERY_HEADS
    k_rows = STEPS * KVH

    def turned(values, scale):
        count = values.shape[0]
        ms = jnp.mean(values * values, axis=1, keepdims=True)
        values = values * lax.rsqrt(ms + EPSILON) * scale
        cosine = jnp.concatenate([cos_ref[...]] * (count // 8), axis=0)
        sine = jnp.concatenate([sin_ref[...]] * (count // 8), axis=0)
        return (values * cosine + pltpu.roll(values, LANES // 2, 1) * sine).astype(jnp.bfloat16)

    loads[1].wait()
    rotated[...] = turned(every[:q_rows], qk_gain_ref[0:1, :])
    new_keys = turned(every[q_rows : q_rows + k_rows], qk_gain_ref[1:2, :])
    new_values = every[q_rows + k_rows :].astype(jnp.bfloat16)

    scaling = 1.0 / math.sqrt(HEAD_SIZE)
    length = length_ref[0]
    loads[4].wait()
    place = t * slots + lax.broadcasted_iota(jnp.int32, (1, slots), 1)
    visible = place < length
    diagonal = lax.broadcasted_iota(jnp.int32, (fine, LANES), 0) == lax.broadcasted_iota(
        jnp.int32, (fine, LANES), 1
    )
    top_row = lax.broadcasted_iota(jnp.int32, (8, LANES), 0) == 0

    def to_row(column):
        return jnp.sum(jnp.where(diagonal, column, 0.0), axis=0, keepdims=True)

    def to_column(row):
        return jnp.sum(jnp.where(diagonal, row, 0.0), axis=1, keepdims=True)

    @pl.loop(0, n)
    def _(i):
        g = lax.rem(t + 1 + i, n)
        query = rotated[pl.ds(pl.multiple_of(g * fine, fine), fine)]
        keys = cache[:, pl.ds(pl.multiple_of(g * LANES, LANES), LANES)]
        values = cache[:, pl.ds(pl.multiple_of(kv_width + g * LANES, LANES), LANES)]
        scores = jnp.where(visible, nt(query, keys) * scaling, -1e30)
        top = jnp.max(scores, axis=1, keepdims=True)
        weights = jnp.where(visible, jnp.exp(scores - top), 0.0)
        count = jnp.sum(weights, axis=1, keepdims=True)
        soft_send[g, :fine] = jnp.dot(
            weights.astype(jnp.bfloat16), values, preferred_element_type=f32
        )
        soft_send[g, fine:] = jnp.where(top_row, to_row(top), to_row(count))

        @pl.when(i < n - 1)
        def _():
            peers_copy(soft_send.at[g], soft_recv.at[t], soft_ssem, soft_rsem, g, t).start()

    own = rotated[pl.ds(pl.multiple_of(t * fine, fine), fine)]
    fresh = nt(own, new_keys) * scaling
    row = lax.broadcasted_iota(jnp.int32, (fine, k_rows), 0)
    col = lax.broadcasted_iota(jnp.int32, (fine, k_rows), 1)
    allowed = jnp.logical_and(col // STEPS == t, col % STEPS <= row % STEPS)
    fresh = jnp.where(allowed, fresh, -1e30)
    fresh_top = jnp.max(fresh, axis=1, keepdims=True)

    soft_recv[t] = soft_send[t]
    for i in range(1, n):
        source = lax.rem(t + i, n)
        peers_copy(
            soft_send.at[source], soft_recv.at[source], soft_ssem, soft_rsem, source, source
        ).wait_recv()
    tops = [to_column(soft_recv[i, fine : fine + 1]) for i in range(n)]
    largest = fresh_top
    for top in tops:
        largest = jnp.maximum(largest, top)
    weights = jnp.where(allowed, jnp.exp(fresh - largest), 0.0)
    denominator = jnp.sum(weights, axis=1, keepdims=True)
    numerator = jnp.dot(weights.astype(jnp.bfloat16), new_values, preferred_element_type=f32)
    for i in range(n):
        factor = jnp.exp(tops[i] - largest)
        denominator += factor * to_column(soft_recv[i, fine + 1 : fine + 2])
        numerator += factor * soft_recv[i, :fine]
    attended = flat(numerator / denominator, fine // STEPS).astype(jnp.bfloat16)

    loads[5].wait()
    loads[6].wait()
    low_out = jnp.dot(attended, down_out[...], preferred_element_type=f32)

    @pl.loop(0, n)
    def _(i):
        target = lax.rem(t + 1 + i, n)
        part = jnp.dot(
            attended, wout[:, pl.ds(pl.multiple_of(target * in_rows, LANES), in_rows)],
            preferred_element_type=f32,
        )
        out_send[target] = jnp.concatenate([tall(part, blocks), low_out], axis=0)

        @pl.when(i < n - 1)
        def _():
            peers_copy(
                out_send.at[target], out_recv.at[t], out_ssem, out_rsem, target, t
            ).start()

    for slot in range(q_chunks, q_chunks + o_chunks):
        pltpu.make_async_copy(up_ref.at[0], up.at[slot], up_rsem.at[slot]).wait()
    summed = out_send[t]
    for i in range(1, n):
        source = lax.rem(t + i, n)
        peers_copy(
            out_send.at[source], out_recv.at[source], out_ssem, out_rsem, source, source
        ).wait_recv()
        summed = summed + out_recv[source]
    base_out = STEPS * blocks
    delta_out = tall(
        nt_fine(summed[base_out:], up[q_chunks:].reshape(in_rows, LANES)), blocks
    )
    hidden = x_rows[:base_out] + summed[:base_out] + ADAPTER_SCALE * delta_out
    spare_out = final_send.shape[0] - base_out
    final_send[...] = jnp.concatenate(
        [hidden, jnp.zeros((spare_out, LANES), f32)], axis=0
    ).astype(jnp.bfloat16)

    @pl.loop(1, n)
    def _(i):
        target = lax.rem(t + i, n)
        peers_copy(final_send, out_ref.at[t], final_ssem, final_rsem, target, t).start()

    out_ref[t] = final_send[...]

    @pl.loop(1, n)
    def _(i):
        source = lax.rem(t + i, n)
        peers_copy(
            final_send, out_ref.at[source], final_ssem, final_rsem, source, source
        ).wait_recv()

    @pl.loop(1, 2 * n)
    def _(i):
        peer = lax.rem(me + i, 2 * n)
        x_copy(peer, me).wait_send()

    for c in range(pieces):
        for fd in range(2):
            target, slot = up_route(c)

            @pl.when(jnp.logical_not(jnp.logical_and(target == t, f == fd)))
            def _():
                up_copy(c, fd).wait_send()

    @pl.loop(1, n)
    def _(i):
        target = lax.rem(t + i, n)
        peers_copy(
            part_send.at[target], part_recv.at[t], part_ssem, part_rsem, target, t
        ).wait_send()
        peers_copy(proj_send, proj_recv.at[t], proj_ssem, proj_rsem, target, t).wait_send()
        peers_copy(
            soft_send.at[target], soft_recv.at[t], soft_ssem, soft_rsem, target, t
        ).wait_send()
        peers_copy(
            out_send.at[target], out_recv.at[t], out_ssem, out_rsem, target, t
        ).wait_send()
        peers_copy(final_send, out_ref.at[t], final_ssem, final_rsem, target, t).wait_send()


def up_to(count, multiple):
    return -(-count // multiple) * multiple


def fused(
    step_token_rows,
    token_embedding_table,
    cached_row_lengths,
    key_value_cache,
    input_norm_gain,
    query_key_gains,
    wqkv,
    wout,
    adapter_down_projections,
    adapter_down_output,
    adapter_up_factors,
):
    n = lax.axis_size("tensor")
    in_rows, projection_width = wqkv.shape
    model_width = wout.shape[1]
    width = projection_width // n
    shard = adapter_up_factors.shape[1]
    chunk = math.gcd(math.gcd(shard, width), in_rows)
    pieces = shard // chunk
    blocks = in_rows // LANES
    heads_here = width // LANES
    bf16, f32 = jnp.bfloat16, jnp.float32

    x_tall = up_to(STEPS * blocks, 16)

    half = HEAD_SIZE // 2
    inverse = ROPE_BASE ** (-(2.0 * jnp.arange(half, dtype=f32)) / HEAD_SIZE)
    position = (cached_row_lengths[0] + jnp.arange(8, dtype=jnp.int32) % STEPS).astype(f32)
    angle = position[:, None] * inverse
    cosine = jnp.cos(angle)
    sine = jnp.sin(angle)
    cosine = jnp.concatenate([cosine, cosine], axis=1)
    sine = jnp.concatenate([-sine, sine], axis=1)
    up = adapter_up_factors.T.reshape(pieces, chunk, LANES)

    part_rows = STEPS * (heads_here + 4)
    proj_rows = up_to(STEPS * heads_here, 16)
    soft_rows = 32 + 8
    out_rows = STEPS * (blocks + 1)
    slots_up = (width + in_rows) // chunk
    vmem = pl.BlockSpec(memory_space=pltpu.VMEM)
    smem = pl.BlockSpec(memory_space=pltpu.SMEM)
    hbm = pl.BlockSpec(memory_space=pl.ANY)
    dma = pltpu.SemaphoreType.DMA
    result = pl.pallas_call(
        lambda *refs: fused_kernel(n, chunk, *refs),
        out_shape=jax.ShapeDtypeStruct((n, x_tall, LANES), bf16),
        in_specs=[smem, smem, vmem, vmem, vmem] + [hbm] * 8,
        out_specs=vmem,
        scratch_shapes=[
            pltpu.VMEM(token_embedding_table.shape, bf16),
            pltpu.VMEM(wqkv.shape, bf16),
            pltpu.VMEM(wout.shape, bf16),
            pltpu.VMEM(key_value_cache.shape[1:], bf16),
            pltpu.VMEM(adapter_down_projections.shape, bf16),
            pltpu.VMEM(adapter_down_output.shape, bf16),
            pltpu.VMEM(query_key_gains.shape, f32),
            pltpu.VMEM((slots_up, chunk, LANES), bf16),
            pltpu.VMEM((2 * n, x_tall, LANES), bf16),
            pltpu.VMEM((2 * n, x_tall, LANES), bf16),
            pltpu.VMEM((x_tall, LANES), f32),
            pltpu.VMEM((n, part_rows, LANES), f32),
            pltpu.VMEM((n, part_rows, LANES), f32),
            pltpu.VMEM((proj_rows, LANES), bf16),
            pltpu.VMEM((n, proj_rows, LANES), bf16),
            pltpu.VMEM((n, STEPS * heads_here, LANES), f32),
            pltpu.VMEM((STEPS * QUERY_HEADS, LANES), bf16),
            pltpu.VMEM((n, soft_rows, LANES), f32),
            pltpu.VMEM((n, soft_rows, LANES), f32),
            pltpu.VMEM((n, out_rows, LANES), f32),
            pltpu.VMEM((n, out_rows, LANES), f32),
            pltpu.VMEM((x_tall, LANES), bf16),
            dma((7,)),
            dma((2 * n,)),
            dma((2 * n,)),
            dma((pieces, 2)),
            dma((slots_up,)),
            dma((slots_up,)),
        ]
        + [dma((n,))] * 10,
        compiler_params=pltpu.CompilerParams(
            collective_id=0, has_side_effects=True, vmem_limit_bytes=60 * 1024 * 1024
        ),
    )(
        step_token_rows,
        cached_row_lengths,
        input_norm_gain.reshape(1, model_width),
        cosine,
        sine,
        query_key_gains,
        up,
        token_embedding_table,
        wqkv,
        wout,
        key_value_cache,
        adapter_down_projections,
        adapter_down_output,
    )
    result = result[:, : STEPS * blocks].reshape(n, blocks, STEPS, LANES)
    return result.transpose(2, 0, 1, 3).reshape(1, STEPS, model_width)


def solution(mesh):
    in_specs = (
        P("group", None),
        P(("fsdp", "tensor"), None),
        P(("group", "fsdp")),
        P(("group", "fsdp"), "tensor", None),
        P(),
        P(),
        P("tensor", None),
        P("tensor", None),
        P("tensor", None),
        P("tensor", None),
        P(None, ("fsdp", "tensor")),
    )
    out_specs = P(("group", "fsdp"), None, None)
    fits = (
        mesh.shape["tensor"] == KVH
        and mesh.shape["fsdp"] == 2
        and HEAD_SIZE == LANES
        and ADAPTER_RANK == LANES
    )
    body = fused if fits else local
    return jax.shard_map(body, mesh=mesh, in_specs=in_specs, out_specs=out_specs, check_vma=False)
```

```python
import math

import jax
import jax.numpy as jnp
from jax import lax
from jax.experimental import pallas as pl
from jax.experimental.pallas import tpu as pltpu
from jax.sharding import PartitionSpec as P

QUERY_HEADS = 64
KVH = 8
HEAD_SIZE = 128
ADAPTER_RANK = 128
STEPS = 4


EPSILON = 1e-06
ROPE_BASE = 1000000.0
ADAPTER_SCALE = 2.0


def combined_all(x, axis, join):
    gathered = jax.tree.map(
        lambda a, kind: lax.all_gather(a.astype(kind), axis),
        x,
        (jnp.bfloat16, jnp.bfloat16, jnp.bfloat16),
    )

    def take(source):
        return jax.tree.map(
            lambda a, own: lax.dynamic_index_in_dim(a, source, 0, False).astype(own.dtype),
            gathered,
            x,
        )

    return lax.fori_loop(
        1, lax.axis_size(axis), lambda source, state: join(state, take(source)), take(0)
    )


def rms_scale(values, gain):
    return values * lax.rsqrt(jnp.mean(values * values, axis=-1, keepdims=True) + EPSILON) * gain


def rotate(values, position):
    half_width = values.shape[-1] // 2
    inverse = ROPE_BASE ** (-(2.0 * jnp.arange(half_width, dtype=jnp.float32)) / values.shape[-1])
    angle = position[..., None] * inverse
    cosine = jnp.cos(angle)
    sine = jnp.sin(angle)
    first_half = values[..., :half_width]
    second_half = values[..., half_width:]
    return jnp.concatenate(
        [first_half * cosine - second_half * sine, second_half * cosine + first_half * sine],
        axis=-1,
    )


def fold_parts(earlier, later):
    top = jnp.maximum(earlier[0], later[0])
    scale_one = jnp.exp(earlier[0] - top)
    scale_two = jnp.exp(later[0] - top)
    return (
        top,
        earlier[1] * scale_one + later[1] * scale_two,
        earlier[2] * scale_one[..., None] + later[2] * scale_two[..., None],
    )


def local(
    step_token_rows,
    token_embedding_table,
    cached_row_lengths,
    key_value_cache,
    input_norm_gain,
    query_key_gains,
    wqkv,
    wout,
    adapter_down_projections,
    adapter_down_output,
    adapter_up_factors,
):
    tensor_count = lax.axis_size("tensor")
    tensor_index = lax.axis_index("tensor")
    fsdp_index = lax.axis_index("fsdp")
    rows_here = cached_row_lengths.shape[0]
    heads_here = QUERY_HEADS // tensor_count
    slots_here = key_value_cache.shape[1]
    groups = QUERY_HEADS // KVH
    query_width = QUERY_HEADS * HEAD_SIZE
    key_value_width = KVH * HEAD_SIZE
    projection_width = wqkv.shape[1]
    model_width = token_embedding_table.shape[1]
    scaling = 1.0 / math.sqrt(HEAD_SIZE)
    adapter_up_whole = lax.all_gather(adapter_up_factors, ("fsdp", "tensor"), axis=1, tiled=True)
    weight_delta = jnp.concatenate(
        [
            jnp.dot(
                adapter_down_projections[:, :ADAPTER_RANK],
                adapter_up_whole[:, :query_width],
                preferred_element_type=jnp.float32,
            ),
            jnp.dot(
                adapter_down_projections[:, ADAPTER_RANK : 2 * ADAPTER_RANK],
                adapter_up_whole[:, query_width : query_width + key_value_width],
                preferred_element_type=jnp.float32,
            ),
            jnp.dot(
                adapter_down_projections[:, 2 * ADAPTER_RANK :],
                adapter_up_whole[:, query_width + key_value_width : projection_width],
                preferred_element_type=jnp.float32,
            ),
        ],
        axis=1,
    )
    merged_projection_weight = (wqkv.astype(jnp.float32) + ADAPTER_SCALE * weight_delta).astype(
        jnp.bfloat16
    )
    output_weight_delta = jnp.dot(
        adapter_down_output,
        adapter_up_whole[:, projection_width:],
        preferred_element_type=jnp.float32,
    )
    merged_output_weight = (wout.astype(jnp.float32) + ADAPTER_SCALE * output_weight_delta).astype(
        jnp.bfloat16
    )
    shard_rows = token_embedding_table.shape[0]
    first_row = (fsdp_index * tensor_count + tensor_index) * shard_rows
    flat_ids = step_token_rows.reshape(-1)
    one_hot = (
        flat_ids[:, None] == first_row + jnp.arange(shard_rows, dtype=jnp.int32)[None, :]
    ).astype(jnp.bfloat16)
    lookup_terms = jnp.dot(one_hot, token_embedding_table, preferred_element_type=jnp.float32)
    looked_up = lax.psum(lookup_terms, ("fsdp", "tensor"))
    embedded = lax.dynamic_slice_in_dim(
        looked_up.reshape(-1, STEPS, model_width), fsdp_index * rows_here, rows_here, 0
    )
    in_rows = wqkv.shape[0]
    cache_keys = key_value_cache[:, :, :key_value_width].reshape(
        rows_here, slots_here, KVH, HEAD_SIZE
    )
    cache_values = key_value_cache[:, :, key_value_width:].reshape(
        rows_here, slots_here, KVH, HEAD_SIZE
    )
    global_slot = tensor_index * slots_here + jnp.arange(slots_here, dtype=jnp.int32)
    visible = global_slot[None, :] < cached_row_lengths[:, None]
    visible_grid = visible[:, None, None, :]

    def own_heads(array):
        return lax.dynamic_slice_in_dim(array, tensor_index * heads_here, heads_here, 1)

    key_list = []
    value_list = []
    results = []
    for decode_step in range(STEPS):
        inputs = embedded[:, decode_step]
        normed = rms_scale(inputs, input_norm_gain.astype(jnp.float32)).astype(jnp.bfloat16)
        normed_slice = lax.dynamic_slice_in_dim(normed, tensor_index * in_rows, in_rows, 1)
        partial_qkv = jnp.dot(
            normed_slice, merged_projection_weight, preferred_element_type=jnp.float32
        )
        projected = lax.psum(partial_qkv, "tensor").astype(jnp.bfloat16)
        queries = (
            projected[:, :query_width]
            .astype(jnp.float32)
            .reshape(rows_here, QUERY_HEADS, HEAD_SIZE)
        )
        new_key = (
            projected[:, query_width : query_width + key_value_width]
            .astype(jnp.float32)
            .reshape(rows_here, KVH, HEAD_SIZE)
        )
        new_value = projected[:, query_width + key_value_width :].reshape(rows_here, KVH, HEAD_SIZE)
        position = (cached_row_lengths + decode_step).astype(jnp.float32)[:, None]
        rotated_query = rotate(rms_scale(queries, query_key_gains[0]), position).astype(
            jnp.bfloat16
        )
        key_list.append(
            rotate(rms_scale(new_key, query_key_gains[1]), position).astype(jnp.bfloat16)
        )
        value_list.append(new_value)
        query_grid = rotated_query.reshape(rows_here, KVH, groups, HEAD_SIZE)
        scores = (
            jnp.einsum(
                "bgrd,bjgd->bgrj", query_grid, cache_keys, preferred_element_type=jnp.float32
            )
            * scaling
        )
        local_max = jnp.max(jnp.where(visible_grid, scores, -1e30), axis=-1)
        weights = jnp.where(visible_grid, jnp.exp(scores - local_max[..., None]), 0.0)
        local_sum = jnp.sum(weights, axis=-1)
        local_acc = jnp.einsum(
            "bgrj,bjgd->bgrd",
            weights.astype(jnp.bfloat16),
            cache_values,
            preferred_element_type=jnp.float32,
        )
        local_max = local_max.reshape(rows_here, QUERY_HEADS)
        local_sum = local_sum.reshape(rows_here, QUERY_HEADS)
        local_acc = local_acc.reshape(rows_here, QUERY_HEADS, HEAD_SIZE)
        merged_parts = combined_all((local_max, local_sum, local_acc), "tensor", fold_parts)
        cache_part = (
            own_heads(merged_parts[0]),
            own_heads(merged_parts[1]),
            own_heads(merged_parts[2]),
        )
        stacked_keys = jnp.stack(key_list, axis=1)
        stacked_values = jnp.stack(value_list, axis=1)
        fresh_scores = (
            jnp.einsum(
                "bgrd,bsgd->bgrs", query_grid, stacked_keys, preferred_element_type=jnp.float32
            )
            * scaling
        )
        fresh_max = jnp.max(fresh_scores, axis=-1)
        fresh_weights = jnp.exp(fresh_scores - fresh_max[..., None])
        fresh_sum = jnp.sum(fresh_weights, axis=-1)
        fresh_acc = jnp.einsum(
            "bgrs,bsgd->bgrd",
            fresh_weights.astype(jnp.bfloat16),
            stacked_values,
            preferred_element_type=jnp.float32,
        )
        fresh_part = (
            own_heads(fresh_max.reshape(rows_here, QUERY_HEADS)),
            own_heads(fresh_sum.reshape(rows_here, QUERY_HEADS)),
            own_heads(fresh_acc.reshape(rows_here, QUERY_HEADS, HEAD_SIZE)),
        )
        combined = fold_parts(cache_part, fresh_part)
        attended = (
            (combined[2] / combined[1][..., None])
            .reshape(rows_here, heads_here * HEAD_SIZE)
            .astype(jnp.bfloat16)
        )
        partial_out = jnp.dot(attended, merged_output_weight, preferred_element_type=jnp.float32)
        summed_out = lax.psum(partial_out, "tensor")
        results.append((inputs + summed_out).astype(jnp.bfloat16))
    return jnp.stack(results, axis=1)


LANES = 128
MESH = pl.DeviceIdType.MESH


def fused_kernel(
    n, chunk,
    ids_ref, length_ref, gain_ref, cos_ref, sin_ref, qk_gain_hbm, up_ref, table_hbm,
    wqkv_hbm, wout_hbm, cache_hbm, down_hbm, down_out_hbm,
    out_ref,
    table, wqkv, wout, cache, down, down_out, qk_gain_ref, up, x_send,
    x_recv, x_rows, part_send, part_recv, proj_send, proj_recv, heads, rotated,
    soft_send, soft_recv, out_send, out_recv, final_send,
    load_sem, x_ssem, x_rsem, up_ssem, up_lsem, up_rsem,
    part_ssem, part_rsem, proj_ssem, proj_rsem, soft_ssem, soft_rsem,
    out_ssem, out_rsem, final_ssem, final_rsem,
):
    f = lax.axis_index("fsdp")
    t = lax.axis_index("tensor")
    me = f * n + t
    in_rows = wqkv.shape[0]
    blocks = in_rows // LANES
    width = wqkv.shape[1] // n
    heads_here = width // LANES
    slots = cache.shape[0]
    kv_width = cache.shape[1] // 2
    model_width = in_rows * n
    fine = 32
    q_chunks = width // chunk
    o_chunks = in_rows // chunk
    all_q = n * q_chunks
    f32 = jnp.float32

    loads = [
        pltpu.make_async_copy(table_hbm, table, load_sem.at[5]),
        pltpu.make_async_copy(qk_gain_hbm, qk_gain_ref, load_sem.at[6]),
        pltpu.make_async_copy(down_hbm, down, load_sem.at[0]),
        pltpu.make_async_copy(wqkv_hbm, wqkv, load_sem.at[1]),
        pltpu.make_async_copy(cache_hbm.at[0], cache, load_sem.at[2]),
        pltpu.make_async_copy(wout_hbm, wout, load_sem.at[3]),
        pltpu.make_async_copy(down_out_hbm, down_out, load_sem.at[4]),
    ]
    for load in loads:
        load.start()

    barrier = pltpu.get_barrier_semaphore()

    @pl.loop(1, 2 * n)
    def _(i):
        peer = lax.rem(me + i, 2 * n)
        pl.semaphore_signal(
            barrier, inc=1, device_id={"fsdp": peer // n, "tensor": lax.rem(peer, n)},
            device_id_type=MESH,
        )

    def x_copy(peer, slot):
        return pltpu.make_async_remote_copy(
            src_ref=x_send.at[peer], dst_ref=x_recv.at[slot],
            send_sem=x_ssem.at[peer], recv_sem=x_rsem.at[slot],
            device_id={"fsdp": peer // n, "tensor": lax.rem(peer, n)}, device_id_type=MESH,
        )

    shard_rows = table.shape[0]
    tokens = lax.broadcasted_iota(jnp.int32, (2 * STEPS, shard_rows), 0)
    local_row = lax.broadcasted_iota(jnp.int32, (2 * STEPS, shard_rows), 1) + me * shard_rows
    wanted = jnp.zeros((2 * STEPS, shard_rows), jnp.int32)
    for k in range(2 * STEPS):
        wanted = jnp.where(tokens == k, ids_ref[k // STEPS, k % STEPS], wanted)
    one_hot = jnp.where(wanted == local_row, 1.0, 0.0).astype(jnp.bfloat16)
    x_pad = jnp.zeros((x_rows.shape[0] - STEPS * blocks, LANES), f32)
    loads[0].wait()

    @pl.loop(0, n)
    def _(i):
        target = lax.rem(t + 1 + i, n)
        found = jnp.dot(
            one_hot, table[:, pl.ds(pl.multiple_of(target * in_rows, LANES), in_rows)],
            preferred_element_type=f32,
        )
        for fd in range(2):
            mine = jnp.concatenate(
                [
                    found[STEPS * fd : STEPS * (fd + 1), LANES * j : LANES * (j + 1)]
                    for j in range(blocks)
                ]
                + [x_pad],
                axis=0,
            )
            x_send[fd * n + target] = mine.astype(jnp.bfloat16)

    pl.semaphore_wait(barrier, 2 * n - 1)

    @pl.loop(1, 2 * n)
    def _(i):
        x_copy(lax.rem(me + i, 2 * n), me).start()

    pieces = up_ref.shape[0]

    def up_route(c):
        g = pieces * me + c
        for_q = g < all_q
        target = jnp.where(for_q, g // q_chunks, (g - all_q) // o_chunks)
        slot = jnp.where(for_q, lax.rem(g, q_chunks), q_chunks + lax.rem(g, o_chunks))
        return target, slot

    def up_copy(c):
        target, slot = up_route(c)
        return pltpu.make_async_remote_copy(
            src_ref=up_ref.at[c], dst_ref=up.at[slot],
            send_sem=up_ssem.at[c], recv_sem=up_rsem.at[slot],
            device_id={"fsdp": f, "tensor": target}, device_id_type=MESH,
        )

    def up_spread(for_q):
        for c in range(pieces):
            target, slot = up_route(c)
            chosen = (pieces * me + c < all_q) == for_q

            @pl.when(jnp.logical_and(chosen, target == t))
            def _():
                pltpu.make_async_copy(up_ref.at[c], up.at[slot], up_rsem.at[slot]).start()

            @pl.when(jnp.logical_and(chosen, target != t))
            def _():
                up_copy(c).start()

    def up_pass(slot):
        return pltpu.make_async_remote_copy(
            src_ref=up.at[slot], dst_ref=up.at[slot],
            send_sem=up_lsem.at[slot], recv_sem=up_rsem.at[slot],
            device_id={"fsdp": 1 - f, "tensor": t}, device_id_type=MESH,
        )

    def up_from_here(slot):
        if slot < q_chunks:
            g = t * q_chunks + slot
        else:
            g = all_q + t * o_chunks + slot - q_chunks
        return g // (pieces * n) == f

    def up_wait(slot):
        pltpu.make_async_copy(up_ref.at[0], up.at[slot], up_rsem.at[slot]).wait()

    def up_forward(span):
        for slot in span:
            @pl.when(up_from_here(slot))
            def _():
                up_wait(slot)
                up_pass(slot).start()

    def up_finish(span):
        for slot in span:
            @pl.when(jnp.logical_not(up_from_here(slot)))
            def _():
                up_wait(slot)

    q_span = range(q_chunks)
    o_span = range(q_chunks, q_chunks + o_chunks)
    up_spread(True)

    def peers_copy(src, dst, ssem, rsem, target, slot):
        return pltpu.make_async_remote_copy(
            src_ref=src, dst_ref=dst, send_sem=ssem.at[target], recv_sem=rsem.at[slot],
            device_id={"fsdp": f, "tensor": target}, device_id_type=MESH,
        )

    x_rows[...] = x_send[me].astype(f32)

    @pl.loop(1, 2 * n)
    def _(i):
        peer = lax.rem(me + i, 2 * n)
        x_copy(peer, peer).wait_recv()
        x_rows[...] += x_recv[peer].astype(f32)

    def flat(values, count):
        return jnp.concatenate(
            [values[STEPS * j : STEPS * (j + 1)] for j in range(count)], axis=1
        )

    def tall(values, count):
        return jnp.concatenate(
            [values[:STEPS, LANES * j : LANES * (j + 1)] for j in range(count)], axis=0
        )

    def nt(a, b):
        return lax.dot_general(a, b, (((1,), (1,)), ((), ())), preferred_element_type=f32)

    def nt_fine(a, b):
        high = a.astype(jnp.bfloat16)
        low = (a - high.astype(f32)).astype(jnp.bfloat16)
        return nt(high, b) + nt(low, b)

    x = flat(x_rows[...], blocks)
    gain = gain_ref[:, pl.ds(pl.multiple_of(t * in_rows, LANES), in_rows)].astype(f32)
    scaled = (x * gain).astype(jnp.bfloat16)
    square = jnp.broadcast_to(jnp.sum(x * x, axis=1, keepdims=True), (STEPS, LANES))
    loads[2].wait()
    low = jnp.dot(scaled, down[...], preferred_element_type=f32)
    part_pad = jnp.zeros((part_send.shape[1] - STEPS * (heads_here + 4), LANES), f32)
    extra = jnp.concatenate([tall(low, 3), square, part_pad], axis=0)
    loads[3].wait()

    @pl.loop(0, n)
    def _(i):
        target = lax.rem(t + 1 + i, n)
        part = jnp.dot(
            scaled, wqkv[:, pl.ds(pl.multiple_of(target * width, LANES), width)],
            preferred_element_type=f32,
        )
        part_send[target] = jnp.concatenate([tall(part, heads_here), extra], axis=0).astype(
            jnp.bfloat16
        )

        @pl.when(i < n - 1)
        def _():
            peers_copy(
                part_send.at[target], part_recv.at[t], part_ssem, part_rsem, target, t
            ).start()

    up_forward(q_span)
    total = part_send[t].astype(f32)
    for i in range(1, n):
        source = lax.rem(t + i, n)
        peers_copy(
            part_send.at[source], part_recv.at[source], part_ssem, part_rsem, source, source
        ).wait_recv()
        total = total + part_recv[source].astype(f32)
    base = STEPS * heads_here
    rate = lax.rsqrt(total[base + 3 * STEPS : base + 4 * STEPS] * (1.0 / model_width) + EPSILON)
    up_finish(q_span)
    factors = total[base : base + 3 * STEPS]
    delta = nt_fine(factors, up[:q_chunks].reshape(width, LANES))
    pieces_out = []
    for j in range(heads_here):
        head = t * heads_here + j
        mine = delta[:, LANES * j : LANES * (j + 1)]
        picked = jnp.where(
            head < QUERY_HEADS,
            mine[:STEPS],
            jnp.where(head < QUERY_HEADS + KVH, mine[STEPS : 2 * STEPS], mine[2 * STEPS :]),
        )
        pieces_out.append((total[STEPS * j : STEPS * (j + 1)] + ADAPTER_SCALE * picked) * rate)
    spare = proj_send.shape[0] - base
    pieces_out.append(jnp.zeros((spare, LANES), f32))
    proj_send[...] = jnp.concatenate(pieces_out, axis=0).astype(jnp.bfloat16)

    @pl.loop(1, n)
    def _(i):
        target = lax.rem(t + i, n)
        peers_copy(proj_send, proj_recv.at[t], proj_ssem, proj_rsem, target, t).start()

    up_spread(False)
    heads[t] = proj_send[...].astype(f32)[:base]

    @pl.loop(1, n)
    def _(i):
        source = lax.rem(t + i, n)
        peers_copy(
            proj_send, proj_recv.at[source], proj_ssem, proj_rsem, source, source
        ).wait_recv()
        heads[source] = proj_recv[source].astype(f32)[:base]

    every = heads[...].reshape(n * base, LANES)
    q_rows = STEPS * QUERY_HEADS
    k_rows = STEPS * KVH

    def turned(values, scale):
        count = values.shape[0]
        ms = jnp.mean(values * values, axis=1, keepdims=True)
        values = values * lax.rsqrt(ms + EPSILON) * scale
        cosine = jnp.concatenate([cos_ref[...]] * (count // 8), axis=0)
        sine = jnp.concatenate([sin_ref[...]] * (count // 8), axis=0)
        return (values * cosine + pltpu.roll(values, LANES // 2, 1) * sine).astype(jnp.bfloat16)

    loads[1].wait()
    rotated[...] = turned(every[:q_rows], qk_gain_ref[0:1, :])
    new_keys = turned(every[q_rows : q_rows + k_rows], qk_gain_ref[1:2, :])
    new_values = every[q_rows + k_rows :].astype(jnp.bfloat16)

    scaling = 1.0 / math.sqrt(HEAD_SIZE)
    length = length_ref[0]
    loads[4].wait()
    place = t * slots + lax.broadcasted_iota(jnp.int32, (1, slots), 1)
    visible = place < length
    diagonal = lax.broadcasted_iota(jnp.int32, (fine, LANES), 0) == lax.broadcasted_iota(
        jnp.int32, (fine, LANES), 1
    )
    top_row = lax.broadcasted_iota(jnp.int32, (8, LANES), 0) == 0

    def to_row(column):
        return jnp.sum(jnp.where(diagonal, column, 0.0), axis=0, keepdims=True)

    def to_column(row):
        return jnp.sum(jnp.where(diagonal, row, 0.0), axis=1, keepdims=True)

    @pl.loop(0, n)
    def _(i):
        g = lax.rem(t + 1 + i, n)
        query = rotated[pl.ds(pl.multiple_of(g * fine, fine), fine)]
        keys = cache[:, pl.ds(pl.multiple_of(g * LANES, LANES), LANES)]
        values = cache[:, pl.ds(pl.multiple_of(kv_width + g * LANES, LANES), LANES)]
        scores = jnp.where(visible, nt(query, keys) * scaling, -1e30)
        top = jnp.max(scores, axis=1, keepdims=True)
        weights = jnp.where(visible, jnp.exp(scores - top), 0.0)
        count = jnp.sum(weights, axis=1, keepdims=True)
        soft_send[g, :fine] = jnp.dot(
            weights.astype(jnp.bfloat16), values, preferred_element_type=f32
        )
        soft_send[g, fine:] = jnp.where(top_row, to_row(top), to_row(count))

        @pl.when(i < n - 1)
        def _():
            peers_copy(soft_send.at[g], soft_recv.at[t], soft_ssem, soft_rsem, g, t).start()

    up_forward(o_span)
    own = rotated[pl.ds(pl.multiple_of(t * fine, fine), fine)]
    fresh = nt(own, new_keys) * scaling
    row = lax.broadcasted_iota(jnp.int32, (fine, k_rows), 0)
    col = lax.broadcasted_iota(jnp.int32, (fine, k_rows), 1)
    allowed = jnp.logical_and(col // STEPS == t, col % STEPS <= row % STEPS)
    fresh = jnp.where(allowed, fresh, -1e30)
    fresh_top = jnp.max(fresh, axis=1, keepdims=True)

    soft_recv[t] = soft_send[t]
    for i in range(1, n):
        source = lax.rem(t + i, n)
        peers_copy(
            soft_send.at[source], soft_recv.at[source], soft_ssem, soft_rsem, source, source
        ).wait_recv()
    tops = [to_column(soft_recv[i, fine : fine + 1]) for i in range(n)]
    largest = fresh_top
    for top in tops:
        largest = jnp.maximum(largest, top)
    weights = jnp.where(allowed, jnp.exp(fresh - largest), 0.0)
    denominator = jnp.sum(weights, axis=1, keepdims=True)
    numerator = jnp.dot(weights.astype(jnp.bfloat16), new_values, preferred_element_type=f32)
    for i in range(n):
        factor = jnp.exp(tops[i] - largest)
        denominator += factor * to_column(soft_recv[i, fine + 1 : fine + 2])
        numerator += factor * soft_recv[i, :fine]
    attended = flat(numerator / denominator, fine // STEPS).astype(jnp.bfloat16)

    loads[5].wait()
    loads[6].wait()
    low_out = jnp.dot(attended, down_out[...], preferred_element_type=f32)

    @pl.loop(0, n)
    def _(i):
        target = lax.rem(t + 1 + i, n)
        part = jnp.dot(
            attended, wout[:, pl.ds(pl.multiple_of(target * in_rows, LANES), in_rows)],
            preferred_element_type=f32,
        )
        out_send[target] = jnp.concatenate([tall(part, blocks), low_out], axis=0)

        @pl.when(i < n - 1)
        def _():
            peers_copy(
                out_send.at[target], out_recv.at[t], out_ssem, out_rsem, target, t
            ).start()

    summed = out_send[t]
    for i in range(1, n):
        source = lax.rem(t + i, n)
        peers_copy(
            out_send.at[source], out_recv.at[source], out_ssem, out_rsem, source, source
        ).wait_recv()
        summed = summed + out_recv[source]
    up_finish(o_span)
    base_out = STEPS * blocks
    delta_out = tall(
        nt_fine(summed[base_out:], up[q_chunks:].reshape(in_rows, LANES)), blocks
    )
    hidden = x_rows[:base_out] + summed[:base_out] + ADAPTER_SCALE * delta_out
    spare_out = final_send.shape[0] - base_out
    final_send[...] = jnp.concatenate(
        [hidden, jnp.zeros((spare_out, LANES), f32)], axis=0
    ).astype(jnp.bfloat16)

    @pl.loop(1, n)
    def _(i):
        target = lax.rem(t + i, n)
        peers_copy(final_send, out_ref.at[t], final_ssem, final_rsem, target, t).start()

    out_ref[t] = final_send[...]

    @pl.loop(1, n)
    def _(i):
        source = lax.rem(t + i, n)
        peers_copy(
            final_send, out_ref.at[source], final_ssem, final_rsem, source, source
        ).wait_recv()

    @pl.loop(1, 2 * n)
    def _(i):
        peer = lax.rem(me + i, 2 * n)
        x_copy(peer, me).wait_send()

    for c in range(pieces):
        @pl.when(up_route(c)[0] != t)
        def _():
            up_copy(c).wait_send()

    for slot in range(q_chunks + o_chunks):
        @pl.when(up_from_here(slot))
        def _():
            up_pass(slot).wait_send()

    @pl.loop(1, n)
    def _(i):
        target = lax.rem(t + i, n)
        peers_copy(
            part_send.at[target], part_recv.at[t], part_ssem, part_rsem, target, t
        ).wait_send()
        peers_copy(proj_send, proj_recv.at[t], proj_ssem, proj_rsem, target, t).wait_send()
        peers_copy(
            soft_send.at[target], soft_recv.at[t], soft_ssem, soft_rsem, target, t
        ).wait_send()
        peers_copy(
            out_send.at[target], out_recv.at[t], out_ssem, out_rsem, target, t
        ).wait_send()
        peers_copy(final_send, out_ref.at[t], final_ssem, final_rsem, target, t).wait_send()


def up_to(count, multiple):
    return -(-count // multiple) * multiple


def fused(
    step_token_rows,
    token_embedding_table,
    cached_row_lengths,
    key_value_cache,
    input_norm_gain,
    query_key_gains,
    wqkv,
    wout,
    adapter_down_projections,
    adapter_down_output,
    adapter_up_factors,
):
    n = lax.axis_size("tensor")
    in_rows, projection_width = wqkv.shape
    model_width = wout.shape[1]
    width = projection_width // n
    shard = adapter_up_factors.shape[1]
    chunk = math.gcd(math.gcd(shard, width), in_rows)
    pieces = shard // chunk
    blocks = in_rows // LANES
    heads_here = width // LANES
    bf16, f32 = jnp.bfloat16, jnp.float32

    x_tall = up_to(STEPS * blocks, 16)

    half = HEAD_SIZE // 2
    inverse = ROPE_BASE ** (-(2.0 * jnp.arange(half, dtype=f32)) / HEAD_SIZE)
    position = (cached_row_lengths[0] + jnp.arange(8, dtype=jnp.int32) % STEPS).astype(f32)
    angle = position[:, None] * inverse
    cosine = jnp.cos(angle)
    sine = jnp.sin(angle)
    cosine = jnp.concatenate([cosine, cosine], axis=1)
    sine = jnp.concatenate([-sine, sine], axis=1)
    up = adapter_up_factors.T.reshape(pieces, chunk, LANES)

    part_rows = up_to(STEPS * (heads_here + 4), 16)
    proj_rows = up_to(STEPS * heads_here, 16)
    soft_rows = 32 + 8
    out_rows = STEPS * (blocks + 1)
    slots_up = (width + in_rows) // chunk
    vmem = pl.BlockSpec(memory_space=pltpu.VMEM)
    smem = pl.BlockSpec(memory_space=pltpu.SMEM)
    hbm = pl.BlockSpec(memory_space=pl.ANY)
    dma = pltpu.SemaphoreType.DMA
    result = pl.pallas_call(
        lambda *refs: fused_kernel(n, chunk, *refs),
        out_shape=jax.ShapeDtypeStruct((n, x_tall, LANES), bf16),
        in_specs=[smem, smem, vmem, vmem, vmem] + [hbm] * 8,
        out_specs=vmem,
        scratch_shapes=[
            pltpu.VMEM(token_embedding_table.shape, bf16),
            pltpu.VMEM(wqkv.shape, bf16),
            pltpu.VMEM(wout.shape, bf16),
            pltpu.VMEM(key_value_cache.shape[1:], bf16),
            pltpu.VMEM(adapter_down_projections.shape, bf16),
            pltpu.VMEM(adapter_down_output.shape, bf16),
            pltpu.VMEM(query_key_gains.shape, f32),
            pltpu.VMEM((slots_up, chunk, LANES), bf16),
            pltpu.VMEM((2 * n, x_tall, LANES), bf16),
            pltpu.VMEM((2 * n, x_tall, LANES), bf16),
            pltpu.VMEM((x_tall, LANES), f32),
            pltpu.VMEM((n, part_rows, LANES), bf16),
            pltpu.VMEM((n, part_rows, LANES), bf16),
            pltpu.VMEM((proj_rows, LANES), bf16),
            pltpu.VMEM((n, proj_rows, LANES), bf16),
            pltpu.VMEM((n, STEPS * heads_here, LANES), f32),
            pltpu.VMEM((STEPS * QUERY_HEADS, LANES), bf16),
            pltpu.VMEM((n, soft_rows, LANES), f32),
            pltpu.VMEM((n, soft_rows, LANES), f32),
            pltpu.VMEM((n, out_rows, LANES), f32),
            pltpu.VMEM((n, out_rows, LANES), f32),
            pltpu.VMEM((x_tall, LANES), bf16),
            dma((7,)),
            dma((2 * n,)),
            dma((2 * n,)),
            dma((pieces,)),
            dma((slots_up,)),
            dma((slots_up,)),
        ]
        + [dma((n,))] * 10,
        compiler_params=pltpu.CompilerParams(
            collective_id=0, has_side_effects=True, vmem_limit_bytes=60 * 1024 * 1024
        ),
    )(
        step_token_rows,
        cached_row_lengths,
        input_norm_gain.reshape(1, model_width),
        cosine,
        sine,
        query_key_gains,
        up,
        token_embedding_table,
        wqkv,
        wout,
        key_value_cache,
        adapter_down_projections,
        adapter_down_output,
    )
    result = result[:, : STEPS * blocks].reshape(n, blocks, STEPS, LANES)
    return result.transpose(2, 0, 1, 3).reshape(1, STEPS, model_width)


def solution(mesh):
    in_specs = (
        P("group", None),
        P(("fsdp", "tensor"), None),
        P(("group", "fsdp")),
        P(("group", "fsdp"), "tensor", None),
        P(),
        P(),
        P("tensor", None),
        P("tensor", None),
        P("tensor", None),
        P("tensor", None),
        P(None, ("fsdp", "tensor")),
    )
    out_specs = P(("group", "fsdp"), None, None)
    fits = (
        mesh.shape["tensor"] == KVH
        and mesh.shape["fsdp"] == 2
        and HEAD_SIZE == LANES
        and ADAPTER_RANK == LANES
    )
    body = fused if fits else local
    return jax.shard_map(body, mesh=mesh, in_specs=in_specs, out_specs=out_specs, check_vma=False)
```

```python
import math

import jax
import jax.numpy as jnp
from jax import lax
from jax.experimental import pallas as pl
from jax.experimental.pallas import tpu as pltpu
from jax.sharding import PartitionSpec as P

QUERY_HEADS = 64
KVH = 8
HEAD_SIZE = 128
ADAPTER_RANK = 128
STEPS = 4


EPSILON = 1e-06
ROPE_BASE = 1000000.0
ADAPTER_SCALE = 2.0


def combined_all(x, axis, join):
    gathered = jax.tree.map(
        lambda a, kind: lax.all_gather(a.astype(kind), axis),
        x,
        (jnp.bfloat16, jnp.bfloat16, jnp.bfloat16),
    )

    def take(source):
        return jax.tree.map(
            lambda a, own: lax.dynamic_index_in_dim(a, source, 0, False).astype(own.dtype),
            gathered,
            x,
        )

    return lax.fori_loop(
        1, lax.axis_size(axis), lambda source, state: join(state, take(source)), take(0)
    )


def rms_scale(values, gain):
    return values * lax.rsqrt(jnp.mean(values * values, axis=-1, keepdims=True) + EPSILON) * gain


def rotate(values, position):
    half_width = values.shape[-1] // 2
    inverse = ROPE_BASE ** (-(2.0 * jnp.arange(half_width, dtype=jnp.float32)) / values.shape[-1])
    angle = position[..., None] * inverse
    cosine = jnp.cos(angle)
    sine = jnp.sin(angle)
    first_half = values[..., :half_width]
    second_half = values[..., half_width:]
    return jnp.concatenate(
        [first_half * cosine - second_half * sine, second_half * cosine + first_half * sine],
        axis=-1,
    )


def fold_parts(earlier, later):
    top = jnp.maximum(earlier[0], later[0])
    scale_one = jnp.exp(earlier[0] - top)
    scale_two = jnp.exp(later[0] - top)
    return (
        top,
        earlier[1] * scale_one + later[1] * scale_two,
        earlier[2] * scale_one[..., None] + later[2] * scale_two[..., None],
    )


def local(
    step_token_rows,
    token_embedding_table,
    cached_row_lengths,
    key_value_cache,
    input_norm_gain,
    query_key_gains,
    wqkv,
    wout,
    adapter_down_projections,
    adapter_down_output,
    adapter_up_factors,
):
    tensor_count = lax.axis_size("tensor")
    tensor_index = lax.axis_index("tensor")
    fsdp_index = lax.axis_index("fsdp")
    rows_here = cached_row_lengths.shape[0]
    heads_here = QUERY_HEADS // tensor_count
    slots_here = key_value_cache.shape[1]
    groups = QUERY_HEADS // KVH
    query_width = QUERY_HEADS * HEAD_SIZE
    key_value_width = KVH * HEAD_SIZE
    projection_width = wqkv.shape[1]
    model_width = token_embedding_table.shape[1]
    scaling = 1.0 / math.sqrt(HEAD_SIZE)
    adapter_up_whole = lax.all_gather(adapter_up_factors, ("fsdp", "tensor"), axis=1, tiled=True)
    weight_delta = jnp.concatenate(
        [
            jnp.dot(
                adapter_down_projections[:, :ADAPTER_RANK],
                adapter_up_whole[:, :query_width],
                preferred_element_type=jnp.float32,
            ),
            jnp.dot(
                adapter_down_projections[:, ADAPTER_RANK : 2 * ADAPTER_RANK],
                adapter_up_whole[:, query_width : query_width + key_value_width],
                preferred_element_type=jnp.float32,
            ),
            jnp.dot(
                adapter_down_projections[:, 2 * ADAPTER_RANK :],
                adapter_up_whole[:, query_width + key_value_width : projection_width],
                preferred_element_type=jnp.float32,
            ),
        ],
        axis=1,
    )
    merged_projection_weight = (wqkv.astype(jnp.float32) + ADAPTER_SCALE * weight_delta).astype(
        jnp.bfloat16
    )
    output_weight_delta = jnp.dot(
        adapter_down_output,
        adapter_up_whole[:, projection_width:],
        preferred_element_type=jnp.float32,
    )
    merged_output_weight = (wout.astype(jnp.float32) + ADAPTER_SCALE * output_weight_delta).astype(
        jnp.bfloat16
    )
    shard_rows = token_embedding_table.shape[0]
    first_row = (fsdp_index * tensor_count + tensor_index) * shard_rows
    flat_ids = step_token_rows.reshape(-1)
    one_hot = (
        flat_ids[:, None] == first_row + jnp.arange(shard_rows, dtype=jnp.int32)[None, :]
    ).astype(jnp.bfloat16)
    lookup_terms = jnp.dot(one_hot, token_embedding_table, preferred_element_type=jnp.float32)
    looked_up = lax.psum(lookup_terms, ("fsdp", "tensor"))
    embedded = lax.dynamic_slice_in_dim(
        looked_up.reshape(-1, STEPS, model_width), fsdp_index * rows_here, rows_here, 0
    )
    in_rows = wqkv.shape[0]
    cache_keys = key_value_cache[:, :, :key_value_width].reshape(
        rows_here, slots_here, KVH, HEAD_SIZE
    )
    cache_values = key_value_cache[:, :, key_value_width:].reshape(
        rows_here, slots_here, KVH, HEAD_SIZE
    )
    global_slot = tensor_index * slots_here + jnp.arange(slots_here, dtype=jnp.int32)
    visible = global_slot[None, :] < cached_row_lengths[:, None]
    visible_grid = visible[:, None, None, :]

    def own_heads(array):
        return lax.dynamic_slice_in_dim(array, tensor_index * heads_here, heads_here, 1)

    key_list = []
    value_list = []
    results = []
    for decode_step in range(STEPS):
        inputs = embedded[:, decode_step]
        normed = rms_scale(inputs, input_norm_gain.astype(jnp.float32)).astype(jnp.bfloat16)
        normed_slice = lax.dynamic_slice_in_dim(normed, tensor_index * in_rows, in_rows, 1)
        partial_qkv = jnp.dot(
            normed_slice, merged_projection_weight, preferred_element_type=jnp.float32
        )
        projected = lax.psum(partial_qkv, "tensor").astype(jnp.bfloat16)
        queries = (
            projected[:, :query_width]
            .astype(jnp.float32)
            .reshape(rows_here, QUERY_HEADS, HEAD_SIZE)
        )
        new_key = (
            projected[:, query_width : query_width + key_value_width]
            .astype(jnp.float32)
            .reshape(rows_here, KVH, HEAD_SIZE)
        )
        new_value = projected[:, query_width + key_value_width :].reshape(rows_here, KVH, HEAD_SIZE)
        position = (cached_row_lengths + decode_step).astype(jnp.float32)[:, None]
        rotated_query = rotate(rms_scale(queries, query_key_gains[0]), position).astype(
            jnp.bfloat16
        )
        key_list.append(
            rotate(rms_scale(new_key, query_key_gains[1]), position).astype(jnp.bfloat16)
        )
        value_list.append(new_value)
        query_grid = rotated_query.reshape(rows_here, KVH, groups, HEAD_SIZE)
        scores = (
            jnp.einsum(
                "bgrd,bjgd->bgrj", query_grid, cache_keys, preferred_element_type=jnp.float32
            )
            * scaling
        )
        local_max = jnp.max(jnp.where(visible_grid, scores, -1e30), axis=-1)
        weights = jnp.where(visible_grid, jnp.exp(scores - local_max[..., None]), 0.0)
        local_sum = jnp.sum(weights, axis=-1)
        local_acc = jnp.einsum(
            "bgrj,bjgd->bgrd",
            weights.astype(jnp.bfloat16),
            cache_values,
            preferred_element_type=jnp.float32,
        )
        local_max = local_max.reshape(rows_here, QUERY_HEADS)
        local_sum = local_sum.reshape(rows_here, QUERY_HEADS)
        local_acc = local_acc.reshape(rows_here, QUERY_HEADS, HEAD_SIZE)
        merged_parts = combined_all((local_max, local_sum, local_acc), "tensor", fold_parts)
        cache_part = (
            own_heads(merged_parts[0]),
            own_heads(merged_parts[1]),
            own_heads(merged_parts[2]),
        )
        stacked_keys = jnp.stack(key_list, axis=1)
        stacked_values = jnp.stack(value_list, axis=1)
        fresh_scores = (
            jnp.einsum(
                "bgrd,bsgd->bgrs", query_grid, stacked_keys, preferred_element_type=jnp.float32
            )
            * scaling
        )
        fresh_max = jnp.max(fresh_scores, axis=-1)
        fresh_weights = jnp.exp(fresh_scores - fresh_max[..., None])
        fresh_sum = jnp.sum(fresh_weights, axis=-1)
        fresh_acc = jnp.einsum(
            "bgrs,bsgd->bgrd",
            fresh_weights.astype(jnp.bfloat16),
            stacked_values,
            preferred_element_type=jnp.float32,
        )
        fresh_part = (
            own_heads(fresh_max.reshape(rows_here, QUERY_HEADS)),
            own_heads(fresh_sum.reshape(rows_here, QUERY_HEADS)),
            own_heads(fresh_acc.reshape(rows_here, QUERY_HEADS, HEAD_SIZE)),
        )
        combined = fold_parts(cache_part, fresh_part)
        attended = (
            (combined[2] / combined[1][..., None])
            .reshape(rows_here, heads_here * HEAD_SIZE)
            .astype(jnp.bfloat16)
        )
        partial_out = jnp.dot(attended, merged_output_weight, preferred_element_type=jnp.float32)
        summed_out = lax.psum(partial_out, "tensor")
        results.append((inputs + summed_out).astype(jnp.bfloat16))
    return jnp.stack(results, axis=1)


LANES = 128
MESH = pl.DeviceIdType.MESH


def fused_kernel(
    n, chunk,
    ids_ref, length_ref, gain_ref, cos_ref, sin_ref, qk_gain_hbm, up_ref, table_hbm,
    wqkv_hbm, wout_hbm, cache_hbm, down_hbm, down_out_hbm,
    out_ref,
    table, wqkv, wout, cache, down, down_out, qk_gain_ref, up, x_send,
    x_recv, x_rows, part_send, part_recv, proj_send, proj_recv, heads, rotated,
    soft_send, soft_recv, out_send, out_recv, final_send,
    load_sem, x_ssem, x_rsem, up_ssem, up_lsem, up_rsem,
    part_ssem, part_rsem, proj_ssem, proj_rsem, soft_ssem, soft_rsem,
    out_ssem, out_rsem, final_ssem, final_rsem,
):
    f = lax.axis_index("fsdp")
    t = lax.axis_index("tensor")
    me = f * n + t
    in_rows = wqkv.shape[0]
    blocks = in_rows // LANES
    width = wqkv.shape[1] // n
    heads_here = width // LANES
    slots = cache.shape[0]
    kv_width = cache.shape[1] // 2
    model_width = in_rows * n
    fine = 32
    q_chunks = width // chunk
    o_chunks = in_rows // chunk
    all_q = n * q_chunks
    f32 = jnp.float32

    loads = [
        pltpu.make_async_copy(table_hbm, table, load_sem.at[5]),
        pltpu.make_async_copy(qk_gain_hbm, qk_gain_ref, load_sem.at[6]),
        pltpu.make_async_copy(down_hbm, down, load_sem.at[0]),
        pltpu.make_async_copy(wqkv_hbm, wqkv, load_sem.at[1]),
        pltpu.make_async_copy(cache_hbm.at[0], cache, load_sem.at[2]),
        pltpu.make_async_copy(wout_hbm, wout, load_sem.at[3]),
        pltpu.make_async_copy(down_out_hbm, down_out, load_sem.at[4]),
    ]
    for load in loads:
        load.start()

    barrier = pltpu.get_barrier_semaphore()

    @pl.loop(1, 2 * n)
    def _(i):
        peer = lax.rem(me + i, 2 * n)
        pl.semaphore_signal(
            barrier, inc=1, device_id={"fsdp": peer // n, "tensor": lax.rem(peer, n)},
            device_id_type=MESH,
        )

    def x_copy(peer, slot):
        return pltpu.make_async_remote_copy(
            src_ref=x_send.at[peer], dst_ref=x_recv.at[slot],
            send_sem=x_ssem.at[peer], recv_sem=x_rsem.at[slot],
            device_id={"fsdp": peer // n, "tensor": lax.rem(peer, n)}, device_id_type=MESH,
        )

    shard_rows = table.shape[0]
    tokens = lax.broadcasted_iota(jnp.int32, (2 * STEPS, shard_rows), 0)
    local_row = lax.broadcasted_iota(jnp.int32, (2 * STEPS, shard_rows), 1) + me * shard_rows
    wanted = jnp.zeros((2 * STEPS, shard_rows), jnp.int32)
    for k in range(2 * STEPS):
        wanted = jnp.where(tokens == k, ids_ref[k // STEPS, k % STEPS], wanted)
    one_hot = jnp.where(wanted == local_row, 1.0, 0.0).astype(jnp.bfloat16)
    x_pad = jnp.zeros((x_rows.shape[0] - STEPS * blocks, LANES), f32)
    loads[0].wait()

    @pl.loop(0, n)
    def _(i):
        target = lax.rem(t + 1 + i, n)
        found = jnp.dot(
            one_hot, table[:, pl.ds(pl.multiple_of(target * in_rows, LANES), in_rows)],
            preferred_element_type=f32,
        )
        for fd in range(2):
            mine = jnp.concatenate(
                [
                    found[STEPS * fd : STEPS * (fd + 1), LANES * j : LANES * (j + 1)]
                    for j in range(blocks)
                ]
                + [x_pad],
                axis=0,
            )
            x_send[fd * n + target] = mine.astype(jnp.bfloat16)

    pl.semaphore_wait(barrier, 2 * n - 1)

    @pl.loop(1, 2 * n)
    def _(i):
        x_copy(lax.rem(me + i, 2 * n), me).start()

    pieces = up_ref.shape[0]

    def up_route(c):
        g = pieces * me + c
        for_q = g < all_q
        target = jnp.where(for_q, g // q_chunks, (g - all_q) // o_chunks)
        slot = jnp.where(for_q, lax.rem(g, q_chunks), q_chunks + lax.rem(g, o_chunks))
        return target, slot

    def up_copy(c):
        target, slot = up_route(c)
        return pltpu.make_async_remote_copy(
            src_ref=up_ref.at[c], dst_ref=up.at[slot],
            send_sem=up_ssem.at[c], recv_sem=up_rsem.at[slot],
            device_id={"fsdp": f, "tensor": target}, device_id_type=MESH,
        )

    def up_spread(for_q):
        for c in range(pieces):
            target, slot = up_route(c)
            chosen = (pieces * me + c < all_q) == for_q

            @pl.when(jnp.logical_and(chosen, target == t))
            def _():
                pltpu.make_async_copy(up_ref.at[c], up.at[slot], up_rsem.at[slot]).start()

            @pl.when(jnp.logical_and(chosen, target != t))
            def _():
                up_copy(c).start()

    def up_pass(slot):
        return pltpu.make_async_remote_copy(
            src_ref=up.at[slot], dst_ref=up.at[slot],
            send_sem=up_lsem.at[slot], recv_sem=up_rsem.at[slot],
            device_id={"fsdp": 1 - f, "tensor": t}, device_id_type=MESH,
        )

    def up_from_here(slot):
        if slot < q_chunks:
            g = t * q_chunks + slot
        else:
            g = all_q + t * o_chunks + slot - q_chunks
        return g // (pieces * n) == f

    def up_wait(slot):
        pltpu.make_async_copy(up_ref.at[0], up.at[slot], up_rsem.at[slot]).wait()

    def up_forward(span):
        for slot in span:
            @pl.when(up_from_here(slot))
            def _():
                up_wait(slot)
                up_pass(slot).start()

    def up_finish(span):
        for slot in span:
            @pl.when(jnp.logical_not(up_from_here(slot)))
            def _():
                up_wait(slot)

    q_span = range(q_chunks)
    o_span = range(q_chunks, q_chunks + o_chunks)
    up_spread(True)

    def peers_copy(src, dst, ssem, rsem, target, slot):
        return pltpu.make_async_remote_copy(
            src_ref=src, dst_ref=dst, send_sem=ssem.at[target], recv_sem=rsem.at[slot],
            device_id={"fsdp": f, "tensor": target}, device_id_type=MESH,
        )

    x_rows[...] = x_send[me].astype(f32)

    @pl.loop(1, 2 * n)
    def _(i):
        peer = lax.rem(me + i, 2 * n)
        x_copy(peer, peer).wait_recv()
        x_rows[...] += x_recv[peer].astype(f32)

    def flat(values, count):
        return jnp.concatenate(
            [values[STEPS * j : STEPS * (j + 1)] for j in range(count)], axis=1
        )

    def tall(values, count):
        return jnp.concatenate(
            [values[:STEPS, LANES * j : LANES * (j + 1)] for j in range(count)], axis=0
        )

    def nt(a, b):
        return lax.dot_general(a, b, (((1,), (1,)), ((), ())), preferred_element_type=f32)

    def nt_fine(a, b):
        high = a.astype(jnp.bfloat16)
        low = (a - high.astype(f32)).astype(jnp.bfloat16)
        return nt(high, b) + nt(low, b)

    x = flat(x_rows[...], blocks)
    gain = gain_ref[:, pl.ds(pl.multiple_of(t * in_rows, LANES), in_rows)].astype(f32)
    scaled = (x * gain).astype(jnp.bfloat16)
    square = jnp.broadcast_to(jnp.sum(x * x, axis=1, keepdims=True), (STEPS, LANES))
    loads[2].wait()
    low = jnp.dot(scaled, down[...], preferred_element_type=f32)
    part_pad = jnp.zeros((part_send.shape[1] - STEPS * (heads_here + 4), LANES), f32)
    extra = jnp.concatenate([tall(low, 3), square, part_pad], axis=0)
    loads[3].wait()

    @pl.loop(0, n)
    def _(i):
        target = lax.rem(t + 1 + i, n)
        part = jnp.dot(
            scaled, wqkv[:, pl.ds(pl.multiple_of(target * width, LANES), width)],
            preferred_element_type=f32,
        )
        part_send[target] = jnp.concatenate([tall(part, heads_here), extra], axis=0).astype(
            jnp.bfloat16
        )

        @pl.when(i < n - 1)
        def _():
            peers_copy(
                part_send.at[target], part_recv.at[t], part_ssem, part_rsem, target, t
            ).start()

    up_forward(q_span)
    total = part_send[t].astype(f32)
    for i in range(1, n):
        source = lax.rem(t + i, n)
        peers_copy(
            part_send.at[source], part_recv.at[source], part_ssem, part_rsem, source, source
        ).wait_recv()
        total = total + part_recv[source].astype(f32)
    base = STEPS * heads_here
    rate = lax.rsqrt(total[base + 3 * STEPS : base + 4 * STEPS] * (1.0 / model_width) + EPSILON)
    up_finish(q_span)
    factors = total[base : base + 3 * STEPS]
    delta = nt_fine(factors, up[:q_chunks].reshape(width, LANES))
    pieces_out = []
    for j in range(heads_here):
        head = t * heads_here + j
        mine = delta[:, LANES * j : LANES * (j + 1)]
        picked = jnp.where(
            head < QUERY_HEADS,
            mine[:STEPS],
            jnp.where(head < QUERY_HEADS + KVH, mine[STEPS : 2 * STEPS], mine[2 * STEPS :]),
        )
        pieces_out.append((total[STEPS * j : STEPS * (j + 1)] + ADAPTER_SCALE * picked) * rate)
    spare = proj_send.shape[0] - base
    pieces_out.append(jnp.zeros((spare, LANES), f32))
    proj_send[...] = jnp.concatenate(pieces_out, axis=0).astype(jnp.bfloat16)

    @pl.loop(1, n)
    def _(i):
        target = lax.rem(t + i, n)
        peers_copy(proj_send, proj_recv.at[t], proj_ssem, proj_rsem, target, t).start()

    up_spread(False)
    heads[t] = proj_send[...].astype(f32)[:base]

    @pl.loop(1, n)
    def _(i):
        source = lax.rem(t + i, n)
        peers_copy(
            proj_send, proj_recv.at[source], proj_ssem, proj_rsem, source, source
        ).wait_recv()
        heads[source] = proj_recv[source].astype(f32)[:base]

    every = heads[...].reshape(n * base, LANES)
    q_rows = STEPS * QUERY_HEADS
    k_rows = STEPS * KVH

    def turned(values, scale):
        count = values.shape[0]
        ms = jnp.mean(values * values, axis=1, keepdims=True)
        values = values * lax.rsqrt(ms + EPSILON) * scale
        cosine = jnp.concatenate([cos_ref[...]] * (count // 8), axis=0)
        sine = jnp.concatenate([sin_ref[...]] * (count // 8), axis=0)
        return (values * cosine + pltpu.roll(values, LANES // 2, 1) * sine).astype(jnp.bfloat16)

    loads[1].wait()
    rotated[...] = turned(every[:q_rows], qk_gain_ref[0:1, :])
    new_keys = turned(every[q_rows : q_rows + k_rows], qk_gain_ref[1:2, :])
    new_values = every[q_rows + k_rows :].astype(jnp.bfloat16)

    scaling = 1.0 / math.sqrt(HEAD_SIZE)
    length = length_ref[0]
    loads[4].wait()
    place = t * slots + lax.broadcasted_iota(jnp.int32, (1, slots), 1)
    visible = place < length
    diagonal = lax.broadcasted_iota(jnp.int32, (fine, LANES), 0) == lax.broadcasted_iota(
        jnp.int32, (fine, LANES), 1
    )
    stat_row = lax.broadcasted_iota(jnp.int32, (16, LANES), 0)

    def three(row):
        high = row.astype(jnp.bfloat16).astype(f32)
        middle = (row - high).astype(jnp.bfloat16).astype(f32)
        return high, middle, row - high - middle

    def to_row(column):
        return jnp.sum(jnp.where(diagonal, column, 0.0), axis=0, keepdims=True)

    def to_column(row):
        return jnp.sum(jnp.where(diagonal, row, 0.0), axis=1, keepdims=True)

    @pl.loop(0, n)
    def _(i):
        g = lax.rem(t + 1 + i, n)
        query = rotated[pl.ds(pl.multiple_of(g * fine, fine), fine)]
        keys = cache[:, pl.ds(pl.multiple_of(g * LANES, LANES), LANES)]
        values = cache[:, pl.ds(pl.multiple_of(kv_width + g * LANES, LANES), LANES)]
        scores = jnp.where(visible, nt(query, keys) * scaling, -1e30)
        top = jnp.max(scores, axis=1, keepdims=True)
        weights = jnp.where(visible, jnp.exp(scores - top), 0.0)
        count = jnp.sum(weights, axis=1, keepdims=True)
        soft_send[g, :fine] = jnp.dot(
            weights.astype(jnp.bfloat16), values, preferred_element_type=f32
        ).astype(jnp.bfloat16)
        stats = jnp.zeros((16, LANES), f32)
        for k, line in enumerate(three(to_row(top)) + three(to_row(count))):
            stats = jnp.where(stat_row == k, line, stats)
        soft_send[g, fine:] = stats.astype(jnp.bfloat16)

        @pl.when(i < n - 1)
        def _():
            peers_copy(soft_send.at[g], soft_recv.at[t], soft_ssem, soft_rsem, g, t).start()

    up_forward(o_span)
    own = rotated[pl.ds(pl.multiple_of(t * fine, fine), fine)]
    fresh = nt(own, new_keys) * scaling
    row = lax.broadcasted_iota(jnp.int32, (fine, k_rows), 0)
    col = lax.broadcasted_iota(jnp.int32, (fine, k_rows), 1)
    allowed = jnp.logical_and(col // STEPS == t, col % STEPS <= row % STEPS)
    fresh = jnp.where(allowed, fresh, -1e30)
    fresh_top = jnp.max(fresh, axis=1, keepdims=True)

    soft_recv[t] = soft_send[t]
    for i in range(1, n):
        source = lax.rem(t + i, n)
        peers_copy(
            soft_send.at[source], soft_recv.at[source], soft_ssem, soft_rsem, source, source
        ).wait_recv()
    stats = [soft_recv[i, fine:].astype(f32) for i in range(n)]
    tops = [to_column(s[0:1] + s[1:2] + s[2:3]) for s in stats]
    largest = fresh_top
    for top in tops:
        largest = jnp.maximum(largest, top)
    weights = jnp.where(allowed, jnp.exp(fresh - largest), 0.0)
    denominator = jnp.sum(weights, axis=1, keepdims=True)
    numerator = jnp.dot(weights.astype(jnp.bfloat16), new_values, preferred_element_type=f32)
    for i in range(n):
        factor = jnp.exp(tops[i] - largest)
        denominator += factor * to_column(stats[i][3:4] + stats[i][4:5] + stats[i][5:6])
        numerator += factor * soft_recv[i, :fine].astype(f32)
    attended = flat(numerator / denominator, fine // STEPS).astype(jnp.bfloat16)

    loads[5].wait()
    loads[6].wait()
    low_out = jnp.dot(attended, down_out[...], preferred_element_type=f32)

    @pl.loop(0, n)
    def _(i):
        target = lax.rem(t + 1 + i, n)
        part = jnp.dot(
            attended, wout[:, pl.ds(pl.multiple_of(target * in_rows, LANES), in_rows)],
            preferred_element_type=f32,
        )
        out_send[target] = jnp.concatenate([tall(part, blocks), low_out], axis=0)

        @pl.when(i < n - 1)
        def _():
            peers_copy(
                out_send.at[target], out_recv.at[t], out_ssem, out_rsem, target, t
            ).start()

    summed = out_send[t]
    for i in range(1, n):
        source = lax.rem(t + i, n)
        peers_copy(
            out_send.at[source], out_recv.at[source], out_ssem, out_rsem, source, source
        ).wait_recv()
        summed = summed + out_recv[source]
    up_finish(o_span)
    base_out = STEPS * blocks
    delta_out = tall(
        nt_fine(summed[base_out:], up[q_chunks:].reshape(in_rows, LANES)), blocks
    )
    hidden = x_rows[:base_out] + summed[:base_out] + ADAPTER_SCALE * delta_out
    spare_out = final_send.shape[0] - base_out
    final_send[...] = jnp.concatenate(
        [hidden, jnp.zeros((spare_out, LANES), f32)], axis=0
    ).astype(jnp.bfloat16)

    @pl.loop(1, n)
    def _(i):
        target = lax.rem(t + i, n)
        peers_copy(final_send, out_ref.at[t], final_ssem, final_rsem, target, t).start()

    out_ref[t] = final_send[...]

    @pl.loop(1, n)
    def _(i):
        source = lax.rem(t + i, n)
        peers_copy(
            final_send, out_ref.at[source], final_ssem, final_rsem, source, source
        ).wait_recv()

    @pl.loop(1, 2 * n)
    def _(i):
        peer = lax.rem(me + i, 2 * n)
        x_copy(peer, me).wait_send()

    for c in range(pieces):
        @pl.when(up_route(c)[0] != t)
        def _():
            up_copy(c).wait_send()

    for slot in range(q_chunks + o_chunks):
        @pl.when(up_from_here(slot))
        def _():
            up_pass(slot).wait_send()

    @pl.loop(1, n)
    def _(i):
        target = lax.rem(t + i, n)
        peers_copy(
            part_send.at[target], part_recv.at[t], part_ssem, part_rsem, target, t
        ).wait_send()
        peers_copy(proj_send, proj_recv.at[t], proj_ssem, proj_rsem, target, t).wait_send()
        peers_copy(
            soft_send.at[target], soft_recv.at[t], soft_ssem, soft_rsem, target, t
        ).wait_send()
        peers_copy(
            out_send.at[target], out_recv.at[t], out_ssem, out_rsem, target, t
        ).wait_send()
        peers_copy(final_send, out_ref.at[t], final_ssem, final_rsem, target, t).wait_send()


def up_to(count, multiple):
    return -(-count // multiple) * multiple


def fused(
    step_token_rows,
    token_embedding_table,
    cached_row_lengths,
    key_value_cache,
    input_norm_gain,
    query_key_gains,
    wqkv,
    wout,
    adapter_down_projections,
    adapter_down_output,
    adapter_up_factors,
):
    n = lax.axis_size("tensor")
    in_rows, projection_width = wqkv.shape
    model_width = wout.shape[1]
    width = projection_width // n
    shard = adapter_up_factors.shape[1]
    chunk = math.gcd(math.gcd(shard, width), in_rows)
    pieces = shard // chunk
    blocks = in_rows // LANES
    heads_here = width // LANES
    bf16, f32 = jnp.bfloat16, jnp.float32

    x_tall = up_to(STEPS * blocks, 16)

    half = HEAD_SIZE // 2
    inverse = ROPE_BASE ** (-(2.0 * jnp.arange(half, dtype=f32)) / HEAD_SIZE)
    position = (cached_row_lengths[0] + jnp.arange(8, dtype=jnp.int32) % STEPS).astype(f32)
    angle = position[:, None] * inverse
    cosine = jnp.cos(angle)
    sine = jnp.sin(angle)
    cosine = jnp.concatenate([cosine, cosine], axis=1)
    sine = jnp.concatenate([-sine, sine], axis=1)
    up = adapter_up_factors.T.reshape(pieces, chunk, LANES)

    part_rows = up_to(STEPS * (heads_here + 4), 16)
    proj_rows = up_to(STEPS * heads_here, 16)
    soft_rows = 32 + 16
    out_rows = STEPS * (blocks + 1)
    slots_up = (width + in_rows) // chunk
    vmem = pl.BlockSpec(memory_space=pltpu.VMEM)
    smem = pl.BlockSpec(memory_space=pltpu.SMEM)
    hbm = pl.BlockSpec(memory_space=pl.ANY)
    dma = pltpu.SemaphoreType.DMA
    result = pl.pallas_call(
        lambda *refs: fused_kernel(n, chunk, *refs),
        out_shape=jax.ShapeDtypeStruct((n, x_tall, LANES), bf16),
        in_specs=[smem, smem, vmem, vmem, vmem] + [hbm] * 8,
        out_specs=vmem,
        scratch_shapes=[
            pltpu.VMEM(token_embedding_table.shape, bf16),
            pltpu.VMEM(wqkv.shape, bf16),
            pltpu.VMEM(wout.shape, bf16),
            pltpu.VMEM(key_value_cache.shape[1:], bf16),
            pltpu.VMEM(adapter_down_projections.shape, bf16),
            pltpu.VMEM(adapter_down_output.shape, bf16),
            pltpu.VMEM(query_key_gains.shape, f32),
            pltpu.VMEM((slots_up, chunk, LANES), bf16),
            pltpu.VMEM((2 * n, x_tall, LANES), bf16),
            pltpu.VMEM((2 * n, x_tall, LANES), bf16),
            pltpu.VMEM((x_tall, LANES), f32),
            pltpu.VMEM((n, part_rows, LANES), bf16),
            pltpu.VMEM((n, part_rows, LANES), bf16),
            pltpu.VMEM((proj_rows, LANES), bf16),
            pltpu.VMEM((n, proj_rows, LANES), bf16),
            pltpu.VMEM((n, STEPS * heads_here, LANES), f32),
            pltpu.VMEM((STEPS * QUERY_HEADS, LANES), bf16),
            pltpu.VMEM((n, soft_rows, LANES), bf16),
            pltpu.VMEM((n, soft_rows, LANES), bf16),
            pltpu.VMEM((n, out_rows, LANES), f32),
            pltpu.VMEM((n, out_rows, LANES), f32),
            pltpu.VMEM((x_tall, LANES), bf16),
            dma((7,)),
            dma((2 * n,)),
            dma((2 * n,)),
            dma((pieces,)),
            dma((slots_up,)),
            dma((slots_up,)),
        ]
        + [dma((n,))] * 10,
        compiler_params=pltpu.CompilerParams(
            collective_id=0, has_side_effects=True, vmem_limit_bytes=60 * 1024 * 1024
        ),
    )(
        step_token_rows,
        cached_row_lengths,
        input_norm_gain.reshape(1, model_width),
        cosine,
        sine,
        query_key_gains,
        up,
        token_embedding_table,
        wqkv,
        wout,
        key_value_cache,
        adapter_down_projections,
        adapter_down_output,
    )
    result = result[:, : STEPS * blocks].reshape(n, blocks, STEPS, LANES)
    return result.transpose(2, 0, 1, 3).reshape(1, STEPS, model_width)


def solution(mesh):
    in_specs = (
        P("group", None),
        P(("fsdp", "tensor"), None),
        P(("group", "fsdp")),
        P(("group", "fsdp"), "tensor", None),
        P(),
        P(),
        P("tensor", None),
        P("tensor", None),
        P("tensor", None),
        P("tensor", None),
        P(None, ("fsdp", "tensor")),
    )
    out_specs = P(("group", "fsdp"), None, None)
    fits = (
        mesh.shape["tensor"] == KVH
        and mesh.shape["fsdp"] == 2
        and HEAD_SIZE == LANES
        and ADAPTER_RANK == LANES
    )
    body = fused if fits else local
    return jax.shard_map(body, mesh=mesh, in_specs=in_specs, out_specs=out_specs, check_vma=False)
```
